32 devices in a mesh: row: 4 (over y, x), col: 8 (over z, core).
Axes of the slice: x: 2, y: 2, z: 4, core: 2. Of those that a mesh axis runs over, the one named last changes fastest.
Arguments:
- segments: float32 [12288, 512], P(('row', 'col')), may hold values from -60 to 60
- exclusion: int32 [1], replicated, may hold values from 1 to 12
Outputs:
- profile: float32 [2, 12288], P(None, ('row', 'col'))
The draws below stay inside these ranges and needn't reach their ends.
All inputs are finite; a program needn't handle non-finite values.
Results may differ from the reference program's by a relative error of at most 0.0005.
Values may be sent and summed in bfloat16 or wider, within the bound.
A program may use at most 192 MiB of HBM per device.

```python
import math
import jax
import jax.numpy as jnp
from jax import lax

SEG_LEN = 512
SEG_DEV = 384
NSEG = 12288


def draw_segments(key, part):
    key = jax.random.fold_in(key, 11)
    subkeys = jax.random.split(key, 7)
    pair_count = NSEG // 2
    shuffle = jax.random.permutation(subkeys[0], NSEG)
    pair_id = jnp.zeros((NSEG,), jnp.int32).at[shuffle].set(jnp.arange(NSEG, dtype=jnp.int32) // 2)
    motifs = jax.random.normal(subkeys[1], (pair_count, SEG_LEN), jnp.float32)
    drawn_fresh = jax.random.normal(subkeys[2], (NSEG + 15, SEG_LEN), jnp.float32)
    jitter = 0.5 * jax.random.normal(subkeys[4], (NSEG, SEG_LEN), jnp.float32)
    amp_low, amp_high = (0.2, 3.0)
    strength = jnp.exp(jax.random.uniform(subkeys[3], (pair_count,), jnp.float32, math.log(amp_low), math.log(amp_high)))
    nearby = drawn_fresh[0:NSEG]
    for shift_by in range(1, 16):
        nearby = nearby + drawn_fresh[shift_by:shift_by + NSEG]
    nearby = 0.25 * nearby
    signal = strength[pair_id][:, None] * motifs[pair_id] + nearby + jitter
    offset_lvl = 3.0 * jax.random.normal(subkeys[5], (NSEG, 1), jnp.float32)
    factor = jnp.exp(jax.random.uniform(subkeys[6], (NSEG, 1), jnp.float32, math.log(0.5), math.log(4.0)))
    return jnp.clip(offset_lvl + factor * signal, -60.0, 60.0)


def setup_inputs(seed: int = 0) -> dict:
    seeds = jax.random.split(jax.random.key(seed), 3)
    segments = draw_segments(jax.random.fold_in(seeds[2], 71), 0)
    exclusion = jax.random.randint(seeds[1], (1,), 1, 13).astype(jnp.int32)
    return {"segments": segments, "exclusion": exclusion}


def statistics(segments):
    seg_len = segments.shape[1]
    average = lax.optimization_barrier(jnp.mean(segments, axis=1))
    centered = segments - average[:, None]
    spread_inv = lax.rsqrt(lax.optimization_barrier(jnp.mean(centered * centered, axis=1)) + 1e-05) * (1.0 / math.sqrt(seg_len))
    return (average, spread_inv)

def normalize(samples, average, spread_inv):
    return ((samples - average[:, None]) * spread_inv[:, None]).astype(jnp.bfloat16)

def reference(segments, exclusion):
    average, spread_inv = statistics(segments)
    normed = normalize(segments, average, spread_inv)
    exclude = exclusion[0]
    row_count = 2 * SEG_DEV
    positions = jnp.arange(NSEG, dtype=jnp.int32)

    def row_minima(blk_index):
        begin_at = (blk_index * row_count).astype(jnp.int32)
        row_data = lax.dynamic_slice_in_dim(normed, begin_at, row_count, 0)
        products = jnp.dot(row_data, normed.T, preferred_element_type=jnp.float32)
        row_pos = begin_at + jnp.arange(row_count, dtype=jnp.int32)
        offset_by = positions[None, :] - row_pos[:, None]
        later = lax.optimization_barrier(jnp.min(jnp.where(offset_by > exclude, 1.0 - products, 4.0), axis=1))
        earlier = lax.optimization_barrier(jnp.min(jnp.where(offset_by < -exclude, 1.0 - products, 4.0), axis=1))
        return jnp.stack([earlier, later])
    minima = lax.map(row_minima, jnp.arange(NSEG // row_count, dtype=jnp.int32))
    return jnp.transpose(minima, (1, 0, 2)).reshape(2, NSEG)
```

```python
import functools
import math

import jax
import jax.numpy as jnp
from jax import lax
from jax.experimental import pallas as pl
from jax.experimental.pallas import tpu as pltpu
from jax.sharding import PartitionSpec as P

MESH = pl.DeviceIdType.MESH
NONE = -3.0
MARGIN = 128
CHUNKS = 4
TILE = 256


def kernel(
    n_row, n_col, seg_ref, exclusion_ref, out_ref, plane, line, row_acc, col_acc,
    col_out, col_in, row_out, row_in, plane_recv, line_recv, col_recv, row_recv,
    data_send, line_send, col_send, row_send,
):
    rows, seg_len = seg_ref.shape
    n_z = n_col // 2
    step = rows // CHUNKS
    my_l = lax.axis_index("row")
    my_col = lax.axis_index("col")
    my_z = my_col // 2
    my_c = my_col % 2
    exclude = exclusion_ref[0]
    shifts = list(range(1, (n_z - 1) // 2 + 1))
    tie = n_z // 2 if n_z % 2 == 0 else 0
    if tie:
        shifts.append(tie)
    upper = my_z // max(tie, 1)
    tie_recv = (my_z % max(tie, 1) + upper) % 2 == 1
    tie_send = (my_z % max(tie, 1) + upper) % 2 == 0
    forwarding = n_row == 4
    if forwarding:
        x_peer = my_l + 1 - 2 * (my_l % 2)
        y_peer = my_l + 2 - 4 * (my_l // 2)
        peers = [x_peer, y_peer, 3 - my_l]
    else:
        peers = [(my_l + o) % n_row for o in range(1, n_row)]

    def device(l, z, c):
        return (l, z * 2 + c)

    barrier = pltpu.get_barrier_semaphore()
    greeted = [device(my_l, my_z, 1 - my_c)]
    for l in peers:
        greeted += [device(l, my_z, my_c), device(l, my_z, 1 - my_c)]
    for d in range(1, n_z):
        greeted.append(device(my_l, (my_z + d) % n_z, my_c))
    for target in greeted:
        pl.semaphore_signal(barrier, inc=1, device_id=target, device_id_type=MESH)

    def normalise(k):
        samples = seg_ref[pl.ds(k * step, step), :]
        average = jnp.mean(samples, axis=1, keepdims=True)
        centered = samples - average
        spread_inv = lax.rsqrt(jnp.mean(centered * centered, axis=1, keepdims=True) + 1e-05) * (
            1.0 / math.sqrt(seg_len)
        )
        plane[my_l, pl.ds(pl.multiple_of(my_c * rows + k * step, 16), step), :] = (
            centered * spread_inv
        ).astype(jnp.bfloat16)

    def part(l, c, k):
        return plane.at[l, pl.ds(pl.multiple_of(c * rows + k * step, 16), step), :]

    started = []

    def send_part(l, c, k, target):
        idx = len(started)
        copy = pltpu.make_async_remote_copy(
            src_ref=part(l, c, k), dst_ref=part(l, c, k), send_sem=data_send.at[idx],
            recv_sem=plane_recv.at[l, c, k], device_id=target, device_id_type=MESH,
        )
        copy.start()
        started.append(copy)

    def await_part(l, c, k):
        pltpu.make_async_remote_copy(
            src_ref=part(l, c, k), dst_ref=part(l, c, k), send_sem=data_send.at[0],
            recv_sem=plane_recv.at[l, c, k], device_id=greeted[0], device_id_type=MESH,
        ).wait_recv()

    def line_copy(i, k):
        d = shifts[i]
        return pltpu.make_async_remote_copy(
            src_ref=part(my_l, my_c, k), dst_ref=line.at[i, pl.ds(k * step, step), :],
            send_sem=line_send.at[i, k], recv_sem=line_recv.at[i, k],
            device_id=device(my_l, (my_z + n_z - d) % n_z, my_c), device_id_type=MESH,
        )

    normalise(0)
    pl.semaphore_wait(barrier, len(greeted))
    sibling = greeted[0]
    for k in range(CHUNKS):
        if k:
            normalise(k)
        for i, d in enumerate(shifts):
            if d != tie:
                line_copy(i, k).start()
        for l in peers[:2] if forwarding else peers:
            send_part(my_l, my_c, k, device(l, my_z, my_c))
        send_part(my_l, my_c, k, sibling)
    if tie:
        @pl.when(tie_send)
        def _():
            for k in range(CHUNKS):
                line_copy(len(shifts) - 1, k).start()

    row_acc[...] = jnp.full(row_acc.shape, NONE, jnp.float32)
    col_acc[...] = jnp.full(col_acc.shape, NONE, jnp.float32)

    def tiles(lhs, slot, z_from, first, count, l, width, with_cols):
        row_start = ((my_l * n_z + z_from) * 2 + my_c) * rows + first
        span = pl.ds(first, count)

        def update_rows(side, values):
            best = values[:, :128]
            for g in range(1, width // 128):
                best = jnp.maximum(best, values[:, g * 128 : (g + 1) * 128])
            row_acc[slot, side, span, :] = jnp.maximum(row_acc[slot, side, span, :], best)

        def update_cols(side, cols, values):
            if with_cols:
                best = jnp.max(values.reshape(count // 8, 8, width), axis=0)
                col_acc[l, side, :, cols] = jnp.maximum(col_acc[l, side, :, cols], best)

        def body(t, carry):
            begin = pl.multiple_of(t * width, width)
            cols = pl.ds(begin, width)
            col_start = (l * n_z + my_z) * 2 * rows + begin

            def products():
                return lax.dot_general(
                    lhs(span), plane[l, cols, :], (((1,), (1,)), ((), ())),
                    preferred_element_type=jnp.float32,
                )

            near = (col_start < row_start + count + MARGIN) & (
                row_start < col_start + width + MARGIN
            )

            @pl.when(near)
            def _():
                p = products()
                apart = (col_start - row_start) + (
                    lax.broadcasted_iota(jnp.int32, (count, width), 1)
                    - lax.broadcasted_iota(jnp.int32, (count, width), 0)
                )
                later = jnp.where(apart > exclude, p, NONE)
                earlier = jnp.where(apart < -exclude, p, NONE)
                update_rows(1, later)
                update_rows(0, earlier)
                update_cols(0, cols, later)
                update_cols(1, cols, earlier)

            @pl.when(jnp.logical_not(near))
            def _():
                p = products()
                side = (col_start > row_start).astype(jnp.int32)
                update_rows(side, p)
                update_cols(1 - side, cols, p)

            return carry

        lax.fori_loop(0, 2 * rows // width, body, 0)

    def own_with(l):
        tiles(lambda span: part_rows(span), 0, my_z, 0, rows, l, TILE, False)

    def part_rows(span):
        return plane[my_l, pl.ds(pl.multiple_of(my_c * rows + span.start, 16), span.size), :]

    def line_with(i, l, first, count, width):
        tiles(
            lambda span: line[i, span, :], i + 1, (my_z + shifts[i]) % n_z,
            first, count, l, width, True,
        )

    def await_line(i, k):
        line_copy(i, k).wait_recv()

    for k in range(CHUNKS):
        await_part(my_l, 1 - my_c, k)
    own_with(my_l)
    if forwarding:
        for k in range(CHUNKS):
            await_part(x_peer, my_c, k)
            if k < CHUNKS // 2:
                send_part(x_peer, my_c, k, device(y_peer, my_z, my_c))
            send_part(x_peer, my_c, k, sibling)
            await_part(y_peer, my_c, k)
            if k >= CHUNKS // 2:
                send_part(y_peer, my_c, k, device(x_peer, my_z, my_c))
            send_part(y_peer, my_c, k, sibling)
        early, late = peers[:2], peers[2:]
    else:
        early, late = peers, []
        for l in early:
            for k in range(CHUNKS):
                await_part(l, my_c, k)
                send_part(l, my_c, k, sibling)
    for l in early:
        for k in range(CHUNKS):
            await_part(l, 1 - my_c, k)
        own_with(l)
    order = [k // 2 + (k % 2) * (CHUNKS // 2) for k in range(CHUNKS)]
    for l in late:
        for k in order[: CHUNKS // 2]:
            await_part(l, my_c, k)
            send_part(l, my_c, k, sibling)
    whole = [i for i, d in enumerate(shifts) if d != tie]
    for i in whole:
        for k in range(CHUNKS):
            await_line(i, k)
        for l in [my_l] + early:
            line_with(i, l, 0, rows, TILE)
    for l in late:
        for k in order[CHUNKS // 2 :]:
            await_part(l, my_c, k)
            send_part(l, my_c, k, sibling)
        for k in range(CHUNKS):
            await_part(l, 1 - my_c, k)
        own_with(l)
        for i in whole:
            line_with(i, l, 0, rows, TILE)

    def send_rows(i):
        for side in range(2):
            row_out[i, side : side + 1, :] = jnp.max(
                row_acc[i + 1, side].T, axis=0, keepdims=True
            )
        row_copy(i).start()

    def row_copy(i):
        return pltpu.make_async_remote_copy(
            src_ref=row_out.at[i], dst_ref=row_in.at[i], send_sem=row_send.at[i],
            recv_sem=row_recv.at[i],
            device_id=device(my_l, (my_z + shifts[i]) % n_z, my_c), device_id_type=MESH,
        )

    for i in whole:
        send_rows(i)
    if tie:
        @pl.when(tie_recv)
        def _():
            i = len(shifts) - 1
            for k in range(CHUNKS):
                await_line(i, k)

                def each(o, carry):
                    line_with(i, o, k * step, step, 2 * rows)
                    return carry

                lax.fori_loop(0, n_row, each, 0)
            send_rows(i)

    def col_copy(l, c):
        return pltpu.make_async_remote_copy(
            src_ref=col_out.at[l, c], dst_ref=col_in.at[my_l, my_c],
            send_sem=col_send.at[l, c], recv_sem=col_recv.at[my_l, my_c],
            device_id=device(l, my_z, c), device_id_type=MESH,
        )

    def await_col(l, c):
        pltpu.make_async_remote_copy(
            src_ref=col_out.at[l, c], dst_ref=col_in.at[l, c],
            send_sem=col_send.at[l, c], recv_sem=col_recv.at[l, c],
            device_id=device(l, my_z, c), device_id_type=MESH,
        ).wait_recv()

    remote = [(l, c) for l in peers for c in (my_c, 1 - my_c)] + [(my_l, 1 - my_c)]
    for l in peers + [my_l]:
        for side in range(2):
            best = jnp.max(col_acc[l, side], axis=0, keepdims=True)
            for c in range(2):
                col_out[l, c, side : side + 1, :] = best[:, c * rows : (c + 1) * rows]
        for c in (1 - my_c,) if l is my_l else (my_c, 1 - my_c):
            col_copy(l, c).start()

    best = jnp.concatenate(
        [jnp.max(row_acc[0, side].T, axis=0, keepdims=True) for side in range(2)], axis=0
    )
    best = jnp.maximum(best, col_out[my_l, my_c])
    for l, c in remote:
        await_col(l, c)
        best = jnp.maximum(best, col_in[l, c])
    for i in whole:
        row_copy(i).wait_recv()
        best = jnp.maximum(best, row_in[i])
    out_ref[...] = 1.0 - best
    if tie:
        @pl.when(tie_send)
        def _():
            i = len(shifts) - 1
            row_copy(i).wait_recv()
            out_ref[...] = jnp.minimum(out_ref[...], 1.0 - row_in[i])

    for copy in started:
        copy.wait_send()
    for i in whole:
        for k in range(CHUNKS):
            line_copy(i, k).wait_send()
        row_copy(i).wait_send()
    for l, c in remote:
        col_copy(l, c).wait_send()
    if tie:
        @pl.when(tie_send)
        def _():
            for k in range(CHUNKS):
                line_copy(len(shifts) - 1, k).wait_send()

        @pl.when(tie_recv)
        def _():
            row_copy(len(shifts) - 1).wait_send()


def shards(segments, exclusion):
    rows, seg_len = segments.shape
    n_row = lax.axis_size("row")
    n_col = lax.axis_size("col")
    n_z = n_col // 2
    slots = n_z // 2
    sends = CHUNKS * (3 * n_row)
    dma = pltpu.SemaphoreType.DMA
    return pl.pallas_call(
        functools.partial(kernel, n_row, n_col),
        out_shape=jax.ShapeDtypeStruct((2, rows), jnp.float32),
        in_specs=[
            pl.BlockSpec(memory_space=pltpu.VMEM),
            pl.BlockSpec(memory_space=pltpu.SMEM),
        ],
        out_specs=pl.BlockSpec(memory_space=pltpu.VMEM),
        scratch_shapes=[
            pltpu.VMEM((n_row, 2 * rows, seg_len), jnp.bfloat16),
            pltpu.VMEM((slots, rows, seg_len), jnp.bfloat16),
            pltpu.VMEM((slots + 1, 2, rows, 128), jnp.float32),
            pltpu.VMEM((n_row, 2, 8, 2 * rows), jnp.float32),
            pltpu.VMEM((n_row, 2, 2, rows), jnp.float32),
            pltpu.VMEM((n_row, 2, 2, rows), jnp.float32),
            pltpu.VMEM((slots, 2, rows), jnp.float32),
            pltpu.VMEM((slots, 2, rows), jnp.float32),
            dma((n_row, 2, CHUNKS)),
            dma((slots, CHUNKS)),
            dma((n_row, 2)),
            dma((slots,)),
            dma((sends,)),
            dma((slots, CHUNKS)),
            dma((n_row, 2)),
            dma((slots,)),
        ],
        compiler_params=pltpu.CompilerParams(
            collective_id=0, has_side_effects=True, vmem_limit_bytes=48 * 1024 * 1024
        ),
        cost_estimate=pl.CostEstimate(
            flops=2 * rows * 2 * rows * n_row * seg_len * (slots + 1),
            bytes_accessed=rows * seg_len * 4,
            transcendentals=0,
        ),
    )(segments, exclusion)


def solution(mesh):
    return jax.shard_map(
        shards,
        mesh=mesh,
        in_specs=(P(("row", "col"), None), P()),
        out_specs=P(None, ("row", "col")),
        check_vma=False,
    )
```

```python
import functools
import math

import jax
import jax.numpy as jnp
from jax import lax
from jax.experimental import pallas as pl
from jax.experimental.pallas import tpu as pltpu
from jax.sharding import PartitionSpec as P

MESH = pl.DeviceIdType.MESH
NONE = -3.0
CHUNKS = 4
TILE = 256


def kernel(
    n_row, n_col, seg_hbm, exclusion_ref, out_ref, seg_ref, in_sem, plane, line, row_acc, col_acc,
    col_out, col_in, row_out, row_in, plane_recv, line_recv, col_recv, row_recv,
    data_send, line_send, col_send, row_send,
):
    rows, seg_len = seg_ref.shape
    n_z = n_col // 2
    step = rows // CHUNKS
    my_l = lax.axis_index("row")
    my_col = lax.axis_index("col")
    my_z = my_col // 2
    my_c = my_col % 2
    loads = [
        pltpu.make_async_copy(
            seg_hbm.at[pl.ds(k * step, step), :], seg_ref.at[pl.ds(k * step, step), :], in_sem.at[k]
        )
        for k in range(CHUNKS)
    ]
    for load in loads:
        load.start()
    shifts = list(range(1, (n_z - 1) // 2 + 1))
    tie = n_z // 2 if n_z % 2 == 0 else 0
    if tie:
        shifts.append(tie)
    upper = my_z // max(tie, 1)
    tie_recv = (my_z % max(tie, 1) + upper) % 2 == 1
    tie_send = (my_z % max(tie, 1) + upper) % 2 == 0
    forwarding = n_row == 4
    if forwarding:
        x_peer = my_l + 1 - 2 * (my_l % 2)
        y_peer = my_l + 2 - 4 * (my_l // 2)
        peers = [x_peer, y_peer, 3 - my_l]
    else:
        peers = [(my_l + o) % n_row for o in range(1, n_row)]

    def device(l, z, c):
        return (l, z * 2 + c)

    barrier = pltpu.get_barrier_semaphore()
    greeted = [device(my_l, my_z, 1 - my_c)]
    for l in peers:
        greeted += [device(l, my_z, my_c), device(l, my_z, 1 - my_c)]
    for d in range(1, n_z):
        greeted.append(device(my_l, (my_z + d) % n_z, my_c))
    for target in greeted:
        pl.semaphore_signal(barrier, inc=1, device_id=target, device_id_type=MESH)

    def normalise(k):
        loads[k].wait()
        samples = seg_ref[pl.ds(k * step, step), :]
        average = jnp.mean(samples, axis=1, keepdims=True)
        centered = samples - average
        spread_inv = lax.rsqrt(jnp.mean(centered * centered, axis=1, keepdims=True) + 1e-05) * (
            1.0 / math.sqrt(seg_len)
        )
        plane[my_l, pl.ds(pl.multiple_of(my_c * rows + k * step, 16), step), :] = (
            centered * spread_inv
        ).astype(jnp.bfloat16)

    def part(l, c, k):
        return plane.at[l, pl.ds(pl.multiple_of(c * rows + k * step, 16), step), :]

    started = []

    def send_part(l, c, k, target):
        idx = len(started)
        copy = pltpu.make_async_remote_copy(
            src_ref=part(l, c, k), dst_ref=part(l, c, k), send_sem=data_send.at[idx],
            recv_sem=plane_recv.at[l, c, k], device_id=target, device_id_type=MESH,
        )
        copy.start()
        started.append(copy)

    def await_part(l, c, k):
        pltpu.make_async_remote_copy(
            src_ref=part(l, c, k), dst_ref=part(l, c, k), send_sem=data_send.at[0],
            recv_sem=plane_recv.at[l, c, k], device_id=greeted[0], device_id_type=MESH,
        ).wait_recv()

    def line_copy(i, k):
        d = shifts[i]
        return pltpu.make_async_remote_copy(
            src_ref=part(my_l, my_c, k), dst_ref=line.at[i, pl.ds(k * step, step), :],
            send_sem=line_send.at[i, k], recv_sem=line_recv.at[i, k],
            device_id=device(my_l, (my_z + n_z - d) % n_z, my_c), device_id_type=MESH,
        )

    normalise(0)
    pl.semaphore_wait(barrier, len(greeted))
    sibling = greeted[0]
    for k in range(CHUNKS):
        if k:
            normalise(k)
        for i, d in enumerate(shifts):
            if d != tie:
                line_copy(i, k).start()
        for l in peers[:2] if forwarding else peers:
            send_part(my_l, my_c, k, device(l, my_z, my_c))
        send_part(my_l, my_c, k, sibling)
    if tie:
        @pl.when(tie_send)
        def _():
            for k in range(CHUNKS):
                line_copy(len(shifts) - 1, k).start()

    row_acc[...] = jnp.full(row_acc.shape, NONE, jnp.float32)
    col_acc[...] = jnp.full(col_acc.shape, NONE, jnp.float32)

    def block(lhs, slot, z_from, first, count, l, width, near, with_cols):
        row_start = ((my_l * n_z + z_from) * 2 + my_c) * rows + first
        span = pl.ds(first, count)

        def update_rows(side, values):
            best = values[:, :128]
            for g in range(1, width // 128):
                best = jnp.maximum(best, values[:, g * 128 : (g + 1) * 128])
            row_acc[slot, side, span, :] = jnp.maximum(row_acc[slot, side, span, :], best)

        def update_cols(side, cols, values):
            if with_cols:
                best = jnp.max(values.reshape(count // 8, 8, width), axis=0)
                col_acc[l, side, :, cols] = jnp.maximum(col_acc[l, side, :, cols], best)

        def products(cols):
            return lax.dot_general(
                lhs(span), plane[l, cols, :], (((1,), (1,)), ((), ())),
                preferred_element_type=jnp.float32,
            )

        def masked():
            for begin in range(0, 2 * rows, width):
                cols = pl.ds(begin, width)
                p = products(cols)
                apart = ((l * n_z + my_z) * 2 * rows + begin - row_start) + (
                    lax.broadcasted_iota(jnp.int32, (count, width), 1)
                    - lax.broadcasted_iota(jnp.int32, (count, width), 0)
                )
                later = jnp.where(apart > exclude, p, NONE)
                earlier = jnp.where(apart < -exclude, p, NONE)
                update_rows(1, later)
                update_rows(0, earlier)
                update_cols(0, cols, later)
                update_cols(1, cols, earlier)

        def plain():
            side = ((l * n_z + my_z) * 2 * rows > row_start).astype(jnp.int32)
            for begin in range(0, 2 * rows, width):
                cols = pl.ds(begin, width)
                p = products(cols)
                update_rows(side, p)
                update_cols(1 - side, cols, p)

        if isinstance(near, bool):
            masked() if near else plain()
        else:
            pl.when(near)(masked)
            pl.when(jnp.logical_not(near))(plain)

    def own_with(l):
        block(part_rows, 0, my_z, 0, rows, l, TILE, n_z == 1 or l is my_l, False)

    def part_rows(span):
        return plane[my_l, pl.ds(pl.multiple_of(my_c * rows + span.start, 16), span.size), :]

    def line_with(i, l, first, count, width):
        d = shifts[i]
        near = False
        if min(d, n_z - d) == 1:
            gap = (l - my_l) * n_z + my_z - (my_z + d) % n_z
            near = (gap >= -1) & (gap <= 1)
        block(
            lambda span: line[i, span, :], i + 1, (my_z + d) % n_z,
            first, count, l, width, near, True,
        )

    def await_line(i, k):
        line_copy(i, k).wait_recv()

    exclude = exclusion_ref[0]
    for k in range(CHUNKS):
        await_part(my_l, 1 - my_c, k)
    own_with(my_l)
    if forwarding:
        for k in range(CHUNKS):
            await_part(x_peer, my_c, k)
            if k < CHUNKS // 2:
                send_part(x_peer, my_c, k, device(y_peer, my_z, my_c))
            send_part(x_peer, my_c, k, sibling)
            await_part(y_peer, my_c, k)
            if k >= CHUNKS // 2:
                send_part(y_peer, my_c, k, device(x_peer, my_z, my_c))
            send_part(y_peer, my_c, k, sibling)
        early, late = peers[:2], peers[2:]
    else:
        early, late = peers, []
        for l in early:
            for k in range(CHUNKS):
                await_part(l, my_c, k)
                send_part(l, my_c, k, sibling)
    for l in early:
        for k in range(CHUNKS):
            await_part(l, 1 - my_c, k)
        own_with(l)
    order = [k // 2 + (k % 2) * (CHUNKS // 2) for k in range(CHUNKS)]
    for l in late:
        for k in order[: CHUNKS // 2]:
            await_part(l, my_c, k)
            send_part(l, my_c, k, sibling)
    whole = [i for i, d in enumerate(shifts) if d != tie]
    for i in whole:
        for k in range(CHUNKS):
            await_line(i, k)
        for l in [my_l] + early:
            line_with(i, l, 0, rows, TILE)
    for l in late:
        for k in order[CHUNKS // 2 :]:
            await_part(l, my_c, k)
            send_part(l, my_c, k, sibling)
        for k in range(CHUNKS):
            await_part(l, 1 - my_c, k)
        own_with(l)
        for i in whole:
            line_with(i, l, 0, rows, TILE)

    def send_rows(i):
        for side in range(2):
            row_out[i, side : side + 1, :] = jnp.max(
                row_acc[i + 1, side].T, axis=0, keepdims=True
            )
        row_copy(i).start()

    def row_copy(i):
        return pltpu.make_async_remote_copy(
            src_ref=row_out.at[i], dst_ref=row_in.at[i], send_sem=row_send.at[i],
            recv_sem=row_recv.at[i],
            device_id=device(my_l, (my_z + shifts[i]) % n_z, my_c), device_id_type=MESH,
        )

    for i in whole:
        send_rows(i)
    own_best = jnp.concatenate(
        [jnp.max(row_acc[0, side].T, axis=0, keepdims=True) for side in range(2)], axis=0
    )
    if tie:
        @pl.when(tie_recv)
        def _():
            i = len(shifts) - 1
            for k in range(CHUNKS):
                await_line(i, k)

                def each(o, carry):
                    line_with(i, o, k * step, step, 2 * rows)
                    return carry

                lax.fori_loop(0, n_row, each, 0)
            send_rows(i)

    def col_copy(l, c):
        return pltpu.make_async_remote_copy(
            src_ref=col_out.at[l, c], dst_ref=col_in.at[my_l, my_c],
            send_sem=col_send.at[l, c], recv_sem=col_recv.at[my_l, my_c],
            device_id=device(l, my_z, c), device_id_type=MESH,
        )

    def await_col(l, c):
        pltpu.make_async_remote_copy(
            src_ref=col_out.at[l, c], dst_ref=col_in.at[l, c],
            send_sem=col_send.at[l, c], recv_sem=col_recv.at[l, c],
            device_id=device(l, my_z, c), device_id_type=MESH,
        ).wait_recv()

    remote = [(l, c) for l in peers for c in (my_c, 1 - my_c)] + [(my_l, 1 - my_c)]
    for l in peers + [my_l]:
        for side in range(2):
            best = jnp.max(col_acc[l, side], axis=0, keepdims=True)
            for c in range(2):
                col_out[l, c, side : side + 1, :] = best[:, c * rows : (c + 1) * rows]
        for c in (1 - my_c,) if l is my_l else (my_c, 1 - my_c):
            col_copy(l, c).start()

    best = jnp.maximum(own_best, col_out[my_l, my_c])
    for l, c in remote:
        await_col(l, c)
        best = jnp.maximum(best, col_in[l, c])
    for i in whole:
        row_copy(i).wait_recv()
        best = jnp.maximum(best, row_in[i])
    out_ref[...] = 1.0 - best
    if tie:
        @pl.when(tie_send)
        def _():
            i = len(shifts) - 1
            row_copy(i).wait_recv()
            out_ref[...] = jnp.minimum(out_ref[...], 1.0 - row_in[i])

    for copy in started:
        copy.wait_send()
    for i in whole:
        for k in range(CHUNKS):
            line_copy(i, k).wait_send()
        row_copy(i).wait_send()
    for l, c in remote:
        col_copy(l, c).wait_send()
    if tie:
        @pl.when(tie_send)
        def _():
            for k in range(CHUNKS):
                line_copy(len(shifts) - 1, k).wait_send()

        @pl.when(tie_recv)
        def _():
            row_copy(len(shifts) - 1).wait_send()


def shards(segments, exclusion):
    rows, seg_len = segments.shape
    n_row = lax.axis_size("row")
    n_col = lax.axis_size("col")
    n_z = n_col // 2
    slots = n_z // 2
    sends = CHUNKS * (3 * n_row)
    dma = pltpu.SemaphoreType.DMA
    return pl.pallas_call(
        functools.partial(kernel, n_row, n_col),
        out_shape=jax.ShapeDtypeStruct((2, rows), jnp.float32),
        in_specs=[
            pl.BlockSpec(memory_space=pl.ANY),
            pl.BlockSpec(memory_space=pltpu.SMEM),
        ],
        out_specs=pl.BlockSpec(memory_space=pltpu.VMEM),
        scratch_shapes=[
            pltpu.VMEM((rows, seg_len), jnp.float32),
            dma((CHUNKS,)),
            pltpu.VMEM((n_row, 2 * rows, seg_len), jnp.bfloat16),
            pltpu.VMEM((slots, rows, seg_len), jnp.bfloat16),
            pltpu.VMEM((slots + 1, 2, rows, 128), jnp.float32),
            pltpu.VMEM((n_row, 2, 8, 2 * rows), jnp.float32),
            pltpu.VMEM((n_row, 2, 2, rows), jnp.float32),
            pltpu.VMEM((n_row, 2, 2, rows), jnp.float32),
            pltpu.VMEM((slots, 2, rows), jnp.float32),
            pltpu.VMEM((slots, 2, rows), jnp.float32),
            dma((n_row, 2, CHUNKS)),
            dma((slots, CHUNKS)),
            dma((n_row, 2)),
            dma((slots,)),
            dma((sends,)),
            dma((slots, CHUNKS)),
            dma((n_row, 2)),
            dma((slots,)),
        ],
        compiler_params=pltpu.CompilerParams(
            collective_id=0, has_side_effects=True, vmem_limit_bytes=60 * 1024 * 1024
        ),
        cost_estimate=pl.CostEstimate(
            flops=2 * rows * 2 * rows * n_row * seg_len * (slots + 1),
            bytes_accessed=rows * seg_len * 4,
            transcendentals=0,
        ),
    )(segments, exclusion)


def solution(mesh):
    return jax.shard_map(
        shards,
        mesh=mesh,
        in_specs=(P(("row", "col"), None), P()),
        out_specs=P(None, ("row", "col")),
        check_vma=False,
    )
```

```python
import functools
import math

import jax
import jax.numpy as jnp
from jax import lax
from jax.experimental import pallas as pl
from jax.experimental.pallas import tpu as pltpu
from jax.sharding import PartitionSpec as P

MESH = pl.DeviceIdType.MESH
NONE = -3.0
CHUNKS = 4
TILE = 256


def kernel(
    n_row, n_col, seg_hbm, exclusion_ref, out_ref, seg_ref, in_sem, plane, line, row_acc, col_acc,
    col_out, col_in, row_out, row_in, plane_recv, line_recv, col_recv, row_recv,
    data_send, line_send, col_send, row_send, pass_send,
):
    rows, seg_len = seg_ref.shape
    n_z = n_col // 2
    step = rows // CHUNKS
    my_l = lax.axis_index("row")
    my_col = lax.axis_index("col")
    my_z = my_col // 2
    my_c = my_col % 2
    loads = [
        pltpu.make_async_copy(
            seg_hbm.at[pl.ds(k * step, step), :], seg_ref.at[pl.ds(k * step, step), :], in_sem.at[k]
        )
        for k in range(CHUNKS)
    ]
    for load in loads:
        load.start()
    shifts = list(range(1, (n_z - 1) // 2 + 1))
    tie = n_z // 2 if n_z % 2 == 0 else 0
    if tie:
        shifts.append(tie)
    upper = my_z // max(tie, 1)
    tie_recv = (my_z % max(tie, 1) + upper) % 2 == 1
    tie_send = (my_z % max(tie, 1) + upper) % 2 == 0
    forwarding = n_row == 4
    passing = n_z == 4
    passes = my_z == 1
    if forwarding:
        x_peer = my_l + 1 - 2 * (my_l % 2)
        y_peer = my_l + 2 - 4 * (my_l // 2)
        peers = [x_peer, y_peer, 3 - my_l]
    else:
        peers = [(my_l + o) % n_row for o in range(1, n_row)]

    def device(l, z, c):
        return (l, z * 2 + c)

    barrier = pltpu.get_barrier_semaphore()
    greeted = [device(my_l, my_z, 1 - my_c)]
    for l in peers:
        greeted += [device(l, my_z, my_c), device(l, my_z, 1 - my_c)]
    for d in range(1, n_z):
        greeted.append(device(my_l, (my_z + d) % n_z, my_c))
    for target in greeted:
        pl.semaphore_signal(barrier, inc=1, device_id=target, device_id_type=MESH)

    def normalise(k):
        loads[k].wait()
        samples = seg_ref[pl.ds(k * step, step), :]
        average = jnp.mean(samples, axis=1, keepdims=True)
        centered = samples - average
        spread_inv = lax.rsqrt(jnp.mean(centered * centered, axis=1, keepdims=True) + 1e-05) * (
            1.0 / math.sqrt(seg_len)
        )
        plane[my_l, pl.ds(pl.multiple_of(my_c * rows + k * step, 16), step), :] = (
            centered * spread_inv
        ).astype(jnp.bfloat16)

    def part(l, c, k):
        return plane.at[l, pl.ds(pl.multiple_of(c * rows + k * step, 16), step), :]

    started = []

    def send_part(l, c, k, target):
        idx = len(started)
        copy = pltpu.make_async_remote_copy(
            src_ref=part(l, c, k), dst_ref=part(l, c, k), send_sem=data_send.at[idx],
            recv_sem=plane_recv.at[l, c, k], device_id=target, device_id_type=MESH,
        )
        copy.start()
        started.append(copy)

    def await_part(l, c, k):
        pltpu.make_async_remote_copy(
            src_ref=part(l, c, k), dst_ref=part(l, c, k), send_sem=data_send.at[0],
            recv_sem=plane_recv.at[l, c, k], device_id=greeted[0], device_id_type=MESH,
        ).wait_recv()

    def line_copy(i, k):
        d = shifts[i]
        return pltpu.make_async_remote_copy(
            src_ref=part(my_l, my_c, k), dst_ref=line.at[i, pl.ds(k * step, step), :],
            send_sem=line_send.at[i, k], recv_sem=line_recv.at[i, k],
            device_id=device(my_l, (my_z + d) % n_z, my_c), device_id_type=MESH,
        )

    def pass_copy(i, k):
        src = line.at[i, pl.ds(k * step, step), :]
        return pltpu.make_async_remote_copy(
            src_ref=src, dst_ref=line.at[1 - i, pl.ds(k * step, step), :],
            send_sem=pass_send.at[i, k], recv_sem=line_recv.at[1 - i, k],
            device_id=device(my_l, 2 - 2 * i, my_c), device_id_type=MESH,
        )

    def pass_on(k):
        if passing:
            @pl.when(passes)
            def _():
                for i in range(2):
                    await_line(i, k)
                    pass_copy(i, k).start()

    normalise(0)
    pl.semaphore_wait(barrier, len(greeted))
    sibling = greeted[0]
    for k in range(CHUNKS):
        if k:
            normalise(k)
        if passing:
            @pl.when(my_z != 3)
            def _():
                line_copy(0, k).start()

            @pl.when(my_z == 3)
            def _():
                line_copy(1, k).start()
        else:
            for i, d in enumerate(shifts):
                if d != tie:
                    line_copy(i, k).start()
        for l in peers[:2] if forwarding else peers:
            send_part(my_l, my_c, k, device(l, my_z, my_c))
        send_part(my_l, my_c, k, sibling)
    if tie and not passing:
        @pl.when(tie_send)
        def _():
            for k in range(CHUNKS):
                line_copy(len(shifts) - 1, k).start()

    row_acc[...] = jnp.full(row_acc.shape, NONE, jnp.float32)
    col_acc[...] = jnp.full(col_acc.shape, NONE, jnp.float32)

    def block(lhs, slot, z_from, first, count, l, width, near, with_cols):
        row_start = ((my_l * n_z + z_from) * 2 + my_c) * rows + first
        span = pl.ds(first, count)

        def update_rows(side, values):
            best = values[:, :128]
            for g in range(1, width // 128):
                best = jnp.maximum(best, values[:, g * 128 : (g + 1) * 128])
            row_acc[slot, side, span, :] = jnp.maximum(row_acc[slot, side, span, :], best)

        def update_cols(side, cols, values):
            if with_cols:
                best = jnp.max(values.reshape(count // 8, 8, width), axis=0)
                col_acc[l, side, :, cols] = jnp.maximum(col_acc[l, side, :, cols], best)

        def products(cols):
            return lax.dot_general(
                lhs(span), plane[l, cols, :], (((1,), (1,)), ((), ())),
                preferred_element_type=jnp.float32,
            )

        def masked():
            for begin in range(0, 2 * rows, width):
                cols = pl.ds(begin, width)
                p = products(cols)
                apart = ((l * n_z + my_z) * 2 * rows + begin - row_start) + (
                    lax.broadcasted_iota(jnp.int32, (count, width), 1)
                    - lax.broadcasted_iota(jnp.int32, (count, width), 0)
                )
                later = jnp.where(apart > exclude, p, NONE)
                earlier = jnp.where(apart < -exclude, p, NONE)
                update_rows(1, later)
                update_rows(0, earlier)
                update_cols(0, cols, later)
                update_cols(1, cols, earlier)

        def plain():
            side = ((l * n_z + my_z) * 2 * rows > row_start).astype(jnp.int32)
            for begin in range(0, 2 * rows, width):
                cols = pl.ds(begin, width)
                p = products(cols)
                update_rows(side, p)
                update_cols(1 - side, cols, p)

        if isinstance(near, bool):
            masked() if near else plain()
        else:
            pl.when(near)(masked)
            pl.when(jnp.logical_not(near))(plain)

    def own_with(l):
        block(part_rows, 0, my_z, 0, rows, l, TILE, n_z == 1 or l is my_l, False)

    def part_rows(span):
        return plane[my_l, pl.ds(pl.multiple_of(my_c * rows + span.start, 16), span.size), :]

    def line_with(i, l, first, count, width):
        d = shifts[i]
        near = False
        if min(d, n_z - d) == 1:
            gap = (l - my_l) * n_z + my_z - (my_z + n_z - d) % n_z
            near = (gap >= -1) & (gap <= 1)
        block(
            lambda span: line[i, span, :], i + 1, (my_z + n_z - d) % n_z,
            first, count, l, width, near, True,
        )

    def await_line(i, k):
        line_copy(i, k).wait_recv()

    exclude = exclusion_ref[0]
    for k in range(CHUNKS):
        await_part(my_l, 1 - my_c, k)
    own_with(my_l)
    if forwarding:
        for k in range(CHUNKS):
            await_part(x_peer, my_c, k)
            if k < CHUNKS // 2:
                send_part(x_peer, my_c, k, device(y_peer, my_z, my_c))
            send_part(x_peer, my_c, k, sibling)
            await_part(y_peer, my_c, k)
            if k >= CHUNKS // 2:
                send_part(y_peer, my_c, k, device(x_peer, my_z, my_c))
            send_part(y_peer, my_c, k, sibling)
            pass_on(k)
        early, late = peers[:2], peers[2:]
    else:
        early, late = peers, []
        for l in early:
            for k in range(CHUNKS):
                await_part(l, my_c, k)
                send_part(l, my_c, k, sibling)
        for k in range(CHUNKS):
            pass_on(k)
    for l in early:
        for k in range(CHUNKS):
            await_part(l, 1 - my_c, k)
        own_with(l)
    order = [k // 2 + (k % 2) * (CHUNKS // 2) for k in range(CHUNKS)]
    for l in late:
        for k in order[: CHUNKS // 2]:
            await_part(l, my_c, k)
            send_part(l, my_c, k, sibling)
    whole = [i for i, d in enumerate(shifts) if d != tie]
    for i in whole:
        for k in range(CHUNKS):
            if passing:
                pl.when(jnp.logical_not(passes))(functools.partial(await_line, i, k))
            else:
                await_line(i, k)
        for l in [my_l] + early:
            line_with(i, l, 0, rows, TILE)
    for l in late:
        for k in order[CHUNKS // 2 :]:
            await_part(l, my_c, k)
            send_part(l, my_c, k, sibling)
        for k in range(CHUNKS):
            await_part(l, 1 - my_c, k)
        own_with(l)
        for i in whole:
            line_with(i, l, 0, rows, TILE)

    def send_rows(i):
        for side in range(2):
            row_out[i, side : side + 1, :] = jnp.max(
                row_acc[i + 1, side].T, axis=0, keepdims=True
            )
        row_copy(i).start()

    def row_copy(i):
        return pltpu.make_async_remote_copy(
            src_ref=row_out.at[i], dst_ref=row_in.at[i], send_sem=row_send.at[i],
            recv_sem=row_recv.at[i],
            device_id=device(my_l, (my_z + n_z - shifts[i]) % n_z, my_c), device_id_type=MESH,
        )

    for i in whole:
        send_rows(i)
    own_best = jnp.concatenate(
        [jnp.max(row_acc[0, side].T, axis=0, keepdims=True) for side in range(2)], axis=0
    )
    if tie:
        @pl.when(tie_recv)
        def _():
            i = len(shifts) - 1
            for k in range(CHUNKS):
                if passing:
                    pl.when(jnp.logical_not(passes))(functools.partial(await_line, i, k))
                else:
                    await_line(i, k)

                def each(o, carry):
                    line_with(i, o, k * step, step, 2 * rows)
                    return carry

                lax.fori_loop(0, n_row, each, 0)
            send_rows(i)

    def col_copy(l, c):
        return pltpu.make_async_remote_copy(
            src_ref=col_out.at[l, c], dst_ref=col_in.at[my_l, my_c],
            send_sem=col_send.at[l, c], recv_sem=col_recv.at[my_l, my_c],
            device_id=device(l, my_z, c), device_id_type=MESH,
        )

    def await_col(l, c):
        pltpu.make_async_remote_copy(
            src_ref=col_out.at[l, c], dst_ref=col_in.at[l, c],
            send_sem=col_send.at[l, c], recv_sem=col_recv.at[l, c],
            device_id=device(l, my_z, c), device_id_type=MESH,
        ).wait_recv()

    remote = [(l, c) for l in peers for c in (my_c, 1 - my_c)] + [(my_l, 1 - my_c)]
    for l in peers + [my_l]:
        for side in range(2):
            best = jnp.max(col_acc[l, side], axis=0, keepdims=True)
            for c in range(2):
                col_out[l, c, side : side + 1, :] = best[:, c * rows : (c + 1) * rows]
        for c in (1 - my_c,) if l is my_l else (my_c, 1 - my_c):
            col_copy(l, c).start()

    best = jnp.maximum(own_best, col_out[my_l, my_c])
    for l, c in remote:
        await_col(l, c)
        best = jnp.maximum(best, col_in[l, c])
    for i in whole:
        row_copy(i).wait_recv()
        best = jnp.maximum(best, row_in[i])
    out_ref[...] = 1.0 - best
    if tie:
        @pl.when(tie_send)
        def _():
            i = len(shifts) - 1
            row_copy(i).wait_recv()
            out_ref[...] = jnp.minimum(out_ref[...], 1.0 - row_in[i])

    for copy in started:
        copy.wait_send()
    for i in whole:
        row_copy(i).wait_send()
    if passing:
        @pl.when(passes)
        def _():
            for i in range(2):
                for k in range(CHUNKS):
                    pass_copy(i, k).wait_send()

        @pl.when(my_z != 3)
        def _():
            for k in range(CHUNKS):
                line_copy(0, k).wait_send()

        @pl.when(my_z == 3)
        def _():
            for k in range(CHUNKS):
                line_copy(1, k).wait_send()
    else:
        for i in whole:
            for k in range(CHUNKS):
                line_copy(i, k).wait_send()
    for l, c in remote:
        col_copy(l, c).wait_send()
    if tie:
        if not passing:
            @pl.when(tie_send)
            def _():
                for k in range(CHUNKS):
                    line_copy(len(shifts) - 1, k).wait_send()

        @pl.when(tie_recv)
        def _():
            row_copy(len(shifts) - 1).wait_send()


def shards(segments, exclusion):
    rows, seg_len = segments.shape
    n_row = lax.axis_size("row")
    n_col = lax.axis_size("col")
    n_z = n_col // 2
    slots = n_z // 2
    sends = CHUNKS * (3 * n_row)
    dma = pltpu.SemaphoreType.DMA
    return pl.pallas_call(
        functools.partial(kernel, n_row, n_col),
        out_shape=jax.ShapeDtypeStruct((2, rows), jnp.float32),
        in_specs=[
            pl.BlockSpec(memory_space=pltpu.HBM),
            pl.BlockSpec(memory_space=pltpu.SMEM),
        ],
        out_specs=pl.BlockSpec(memory_space=pltpu.VMEM),
        scratch_shapes=[
            pltpu.VMEM((rows, seg_len), jnp.float32),
            dma((CHUNKS,)),
            pltpu.VMEM((n_row, 2 * rows, seg_len), jnp.bfloat16),
            pltpu.VMEM((slots, rows, seg_len), jnp.bfloat16),
            pltpu.VMEM((slots + 1, 2, rows, 128), jnp.float32),
            pltpu.VMEM((n_row, 2, 8, 2 * rows), jnp.float32),
            pltpu.VMEM((n_row, 2, 2, rows), jnp.float32),
            pltpu.VMEM((n_row, 2, 2, rows), jnp.float32),
            pltpu.VMEM((slots, 2, rows), jnp.float32),
            pltpu.VMEM((slots, 2, rows), jnp.float32),
            dma((n_row, 2, CHUNKS)),
            dma((slots, CHUNKS)),
            dma((n_row, 2)),
            dma((slots,)),
            dma((sends,)),
            dma((slots, CHUNKS)),
            dma((n_row, 2)),
            dma((slots,)),
            dma((2, CHUNKS)),
        ],
        compiler_params=pltpu.CompilerParams(
            collective_id=0, has_side_effects=True, vmem_limit_bytes=48 * 1024 * 1024
        ),
        cost_estimate=pl.CostEstimate(
            flops=2 * rows * 2 * rows * n_row * seg_len * (slots + 1),
            bytes_accessed=rows * seg_len * 4,
            transcendentals=0,
        ),
    )(segments, exclusion)


def solution(mesh):
    return jax.shard_map(
        shards,
        mesh=mesh,
        in_specs=(P(("row", "col"), None), P()),
        out_specs=P(None, ("row", "col")),
        check_vma=False,
    )
```

```python
import functools
import math

import jax
import jax.numpy as jnp
from jax import lax
from jax.experimental import pallas as pl
from jax.experimental.pallas import tpu as pltpu
from jax.sharding import PartitionSpec as P

MESH = pl.DeviceIdType.MESH
NONE = -3.0
CHUNKS = 4
TILE = 256


def kernel(
    n_row, n_col, seg_hbm, exclusion_ref, out_ref, seg_ref, in_sem, plane, line, line_acc,
    plane_acc, tie_rows, tie_cols, line_out, line_in, plane_out, plane_in, plane_recv, line_recv,
    msg_plane_recv, msg_line_recv, data_send, line_send, pair_send, pass_send, msg_plane_send,
    msg_line_send,
):
    rows, seg_len = seg_ref.shape
    n_z = n_col // 2
    step = rows // CHUNKS
    my_l = lax.axis_index("row")
    my_col = lax.axis_index("col")
    my_z = my_col // 2
    my_c = my_col % 2
    loads = [
        pltpu.make_async_copy(
            seg_hbm.at[pl.ds(k * step, step), :], seg_ref.at[pl.ds(k * step, step), :], in_sem.at[k]
        )
        for k in range(CHUNKS)
    ]
    for load in loads:
        load.start()
    shifts = list(range(1, (n_z - 1) // 2 + 1))
    tie = n_z // 2 if n_z % 2 == 0 else 0
    upper = my_z // max(tie, 1)
    tie_recv = (my_z % max(tie, 1) + upper) % 2 == 1
    tie_send = (my_z % max(tie, 1) + upper) % 2 == 0
    forwarding = n_row == 4
    passing = n_z == 4
    passes = my_z == 1
    if forwarding:
        x_peer = my_l + 1 - 2 * (my_l % 2)
        y_peer = my_l + 2 - 4 * (my_l // 2)
        peers = [x_peer, y_peer, 3 - my_l]
    else:
        peers = [(my_l + o) % n_row for o in range(1, n_row)]

    def device(l, z, c):
        return (l, z * 2 + c)

    barrier = pltpu.get_barrier_semaphore()
    sibling = device(my_l, my_z, 1 - my_c)
    greeted = [sibling] + [device(l, my_z, my_c) for l in peers]
    for d in range(1, n_z):
        greeted.append(device(my_l, (my_z + d) % n_z, my_c))
        greeted.append(device(my_l, (my_z + d) % n_z, 1 - my_c))
    for target in greeted:
        pl.semaphore_signal(barrier, inc=1, device_id=target, device_id_type=MESH)

    def half(c, k):
        return pl.ds(pl.multiple_of(c * rows + k * step, 16), step)

    def normalise(k):
        loads[k].wait()
        span = pl.ds(k * step, step)
        samples = seg_ref[span, :]
        average = jnp.mean(samples, axis=1, keepdims=True)
        centered = samples - average
        spread_inv = lax.rsqrt(jnp.mean(centered * centered, axis=1, keepdims=True) + 1e-05) * (
            1.0 / math.sqrt(seg_len)
        )
        normed = (centered * spread_inv).astype(jnp.bfloat16)
        plane[my_l, span, :] = normed
        line[0, half(my_c, k), :] = normed

    started = []

    def plane_copy(l, k, send_sem, target):
        part = plane.at[l, pl.ds(k * step, step), :]
        return pltpu.make_async_remote_copy(
            src_ref=part, dst_ref=part, send_sem=send_sem,
            recv_sem=plane_recv.at[l, k], device_id=target, device_id_type=MESH,
        )

    def send_part(l, k, target):
        copy = plane_copy(l, k, data_send.at[len(started)], device(target, my_z, my_c))
        copy.start()
        started.append(copy)

    def await_part(l, k):
        plane_copy(l, k, data_send.at[0], sibling).wait_recv()

    def line_copy(s, k):
        return pltpu.make_async_remote_copy(
            src_ref=plane.at[my_l, pl.ds(k * step, step), :], dst_ref=line.at[s, half(my_c, k), :],
            send_sem=line_send.at[s, k], recv_sem=line_recv.at[s, my_c, k],
            device_id=device(my_l, (my_z + s) % n_z, my_c), device_id_type=MESH,
        )

    def pair_copy(s, k):
        part = line.at[s, half(my_c, k), :]
        return pltpu.make_async_remote_copy(
            src_ref=part, dst_ref=part, send_sem=pair_send.at[s, k],
            recv_sem=line_recv.at[s, my_c, k], device_id=sibling, device_id_type=MESH,
        )

    def await_line(s, c, k):
        part = line.at[s, half(c, k), :]
        pltpu.make_async_remote_copy(
            src_ref=part, dst_ref=part, send_sem=pair_send.at[s, k],
            recv_sem=line_recv.at[s, c, k], device_id=sibling, device_id_type=MESH,
        ).wait_recv()

    def pass_copy(s, k):
        return pltpu.make_async_remote_copy(
            src_ref=line.at[s, half(my_c, k), :], dst_ref=line.at[3 - s, half(my_c, k), :],
            send_sem=pass_send.at[s - 1, k], recv_sem=line_recv.at[3 - s, my_c, k],
            device_id=device(my_l, 4 - 2 * s, my_c), device_id_type=MESH,
        )

    def take_line(s, k):
        await_line(s, my_c, k)
        pair_copy(s, k).start()

    normalise(0)
    pl.semaphore_wait(barrier, len(greeted))
    for k in range(CHUNKS):
        if k:
            normalise(k)
        if passing:
            pl.when(my_z != 3)(lambda: line_copy(1, k).start())
            pl.when(my_z == 3)(lambda: line_copy(2, k).start())
        else:
            for s in shifts:
                line_copy(s, k).start()
        for l in peers[:2] if forwarding else peers:
            send_part(my_l, k, l)
        pair_copy(0, k).start()
    if tie and not passing:
        @pl.when(tie_send)
        def _():
            for k in range(CHUNKS):
                line_copy(tie, k).start()

    line_acc[...] = jnp.full(line_acc.shape, NONE, jnp.float32)
    plane_acc[...] = jnp.full(plane_acc.shape, NONE, jnp.float32)
    tie_rows[...] = jnp.full(tie_rows.shape, NONE, jnp.float32)
    tie_cols[...] = jnp.full(tie_cols.shape, NONE, jnp.float32)
    exclude = exclusion_ref[0]

    def dot(a, b):
        return lax.dot_general(
            a, b, (((1,), (1,)), ((), ())), preferred_element_type=jnp.float32
        )

    def lanes(values):
        best = values[:, :128]
        for g in range(1, values.shape[1] // 128):
            best = jnp.maximum(best, values[:, g * 128 : (g + 1) * 128])
        return best

    def sublanes(values):
        return jnp.max(values.reshape(values.shape[0] // 8, 8, values.shape[1]), axis=0)

    def gap_of(s, l):
        return (l - my_l) * n_z + my_z - (my_z + n_z - s) % n_z

    def block(s, l):
        gap = gap_of(s, l)

        def keep(side, cols, values):
            line_acc[s, side, :, cols] = jnp.maximum(line_acc[s, side, :, cols], sublanes(values))
            if s:
                plane_acc[l, 1 - side] = jnp.maximum(plane_acc[l, 1 - side], lanes(values))

        def masked():
            for begin in range(0, 2 * rows, TILE):
                cols = pl.ds(begin, TILE)
                p = dot(plane[l], line[s, cols, :])
                apart = (gap * 2 * rows + my_c * rows - begin) + (
                    lax.broadcasted_iota(jnp.int32, p.shape, 0)
                    - lax.broadcasted_iota(jnp.int32, p.shape, 1)
                )
                keep(1, cols, jnp.where(apart > exclude, p, NONE))
                keep(0, cols, jnp.where(apart < -exclude, p, NONE))

        def plain():
            side = (gap > 0).astype(jnp.int32)
            for begin in range(0, 2 * rows, TILE):
                cols = pl.ds(begin, TILE)
                keep(side, cols, dot(plane[l], line[s, cols, :]))

        if s == 0:
            masked() if n_z == 1 or l is my_l else plain()
        elif min(s, n_z - s) == 1:
            near = (gap >= -1) & (gap <= 1)
            pl.when(near)(masked)
            pl.when(jnp.logical_not(near))(plain)
        else:
            plain()

    for k in range(CHUNKS):
        await_line(0, 1 - my_c, k)
    block(0, my_l)
    if forwarding:
        for k in range(CHUNKS):
            await_part(x_peer, k)
            if k < CHUNKS // 2:
                send_part(x_peer, k, y_peer)
            await_part(y_peer, k)
            if k >= CHUNKS // 2:
                send_part(y_peer, k, x_peer)
            if passing:
                @pl.when(my_z != 0)
                def _():
                    take_line(1, k)

                @pl.when(passes)
                def _():
                    pass_copy(1, k).start()
                    take_line(2, k)
                    pass_copy(2, k).start()
        early, late = peers[:2], peers[2:]
    else:
        early, late = peers, []
        for l in early:
            for k in range(CHUNKS):
                await_part(l, k)
        if passing:
            for k in range(CHUNKS):
                @pl.when(my_z != 0)
                def _():
                    take_line(1, k)

                @pl.when(passes)
                def _():
                    pass_copy(1, k).start()
                    take_line(2, k)
                    pass_copy(2, k).start()
    for l in early:
        block(0, l)
    for s in shifts:
        for k in range(CHUNKS):
            if passing:
                pl.when(my_z == 0)(functools.partial(take_line, s, k))
            else:
                take_line(s, k)
        for k in range(CHUNKS):
            await_line(s, 1 - my_c, k)
        for l in [my_l] + early:
            block(s, l)
    for l in late:
        for k in range(CHUNKS):
            await_part(l, k)
        for s in [0] + shifts:
            block(s, l)

    def msg_line_copy(s, c):
        return pltpu.make_async_remote_copy(
            src_ref=line_out.at[s, c], dst_ref=line_in.at[s, my_c],
            send_sem=msg_line_send.at[s, c], recv_sem=msg_line_recv.at[s, my_c],
            device_id=device(my_l, (my_z + n_z - s) % n_z, c), device_id_type=MESH,
        )

    def await_msg_line(s, c):
        pltpu.make_async_remote_copy(
            src_ref=line_out.at[s, c], dst_ref=line_in.at[s, c],
            send_sem=msg_line_send.at[s, c], recv_sem=msg_line_recv.at[s, c],
            device_id=sibling, device_id_type=MESH,
        ).wait_recv()

    for s in [0] + shifts:
        for side in range(2):
            best = jnp.max(line_acc[s, side], axis=0, keepdims=True)
            for c in range(2):
                line_out[s, c, side : side + 1, :] = best[:, c * rows : (c + 1) * rows]
        for c in (my_c, 1 - my_c) if s else (1 - my_c,):
            msg_line_copy(s, c).start()
    if shifts:
        for l in range(n_row):
            for side in range(2):
                plane_out[l, side : side + 1, :] = jnp.max(
                    plane_acc[l, side].T, axis=0, keepdims=True
                )
    else:
        plane_out[...] = jnp.full(plane_out.shape, NONE, jnp.float32)

    if tie:
        @pl.when(tie_recv)
        def _():
            done = 0
            for k in range(CHUNKS):
                if passing:
                    pl.when(jnp.logical_not(passes))(functools.partial(take_line, tie, k))
                else:
                    take_line(tie, k)
                await_line(tie, 1 - my_c, k)
                spans = [pl.ds(c * rows + k * step, step) for c in range(2)]
                data = jnp.concatenate([line[tie, span, :] for span in spans], axis=0)
                for l in range(n_row):
                    p = dot(data, plane[l])
                    gap = gap_of(tie, l)

                    def keep(side, line_values, plane_values):
                        best = lanes(line_values)
                        for c, span in enumerate(spans):
                            tie_rows[side, span, :] = jnp.maximum(
                                tie_rows[side, span, :], best[c * step : (c + 1) * step]
                            )
                        tie_cols[l, 1 - side] = jnp.maximum(
                            tie_cols[l, 1 - side], sublanes(plane_values)
                        )

                    if min(tie, n_z - tie) == 1:
                        index = lax.broadcasted_iota(jnp.int32, p.shape, 0)
                        index = jnp.where(index >= step, index + (rows - step), index) + k * step
                        apart = (gap * 2 * rows + my_c * rows) + (
                            lax.broadcasted_iota(jnp.int32, p.shape, 1) - index
                        )
                        later = jnp.where(apart > exclude, p, NONE)
                        earlier = jnp.where(apart < -exclude, p, NONE)
                        keep(1, later, later)
                        keep(0, earlier, earlier)
                    else:
                        keep((gap > 0).astype(jnp.int32), p, p)
                upto = (k + 1) * step // 128 * 128
                if upto > done:
                    for c in range(2):
                        for side in range(2):
                            line_out[tie, c, side : side + 1, done:upto] = jnp.max(
                                tie_rows[side, c * rows + done : c * rows + upto, :].T,
                                axis=0, keepdims=True,
                            )
                    done = upto
            for c in (my_c, 1 - my_c):
                msg_line_copy(tie, c).start()
            for l in range(n_row):
                for side in range(2):
                    plane_out[l, side : side + 1, :] = jnp.maximum(
                        plane_out[l, side : side + 1, :],
                        jnp.max(tie_cols[l, side], axis=0, keepdims=True),
                    )

    def msg_plane_copy(l):
        return pltpu.make_async_remote_copy(
            src_ref=plane_out.at[l], dst_ref=plane_in.at[my_l],
            send_sem=msg_plane_send.at[l], recv_sem=msg_plane_recv.at[my_l],
            device_id=device(l, my_z, my_c), device_id_type=MESH,
        )

    def await_msg_plane(l):
        pltpu.make_async_remote_copy(
            src_ref=plane_out.at[l], dst_ref=plane_in.at[l],
            send_sem=msg_plane_send.at[l], recv_sem=msg_plane_recv.at[l],
            device_id=sibling, device_id_type=MESH,
        ).wait_recv()

    for l in peers:
        msg_plane_copy(l).start()
    best = jnp.maximum(line_out[0, my_c], plane_out[my_l])
    await_msg_line(0, 1 - my_c)
    best = jnp.maximum(best, line_in[0, 1 - my_c])
    for s in shifts:
        for c in range(2):
            await_msg_line(s, c)
            best = jnp.maximum(best, line_in[s, c])
    for l in peers:
        await_msg_plane(l)
        best = jnp.maximum(best, plane_in[l])
    out_ref[...] = 1.0 - best
    if tie:
        @pl.when(tie_send)
        def _():
            for c in range(2):
                await_msg_line(tie, c)
            out_ref[...] = jnp.minimum(
                out_ref[...], 1.0 - jnp.maximum(line_in[tie, 0], line_in[tie, 1])
            )

    for copy in started:
        copy.wait_send()
    for k in range(CHUNKS):
        pair_copy(0, k).wait_send()
        for s in shifts:
            pair_copy(s, k).wait_send()
    msg_line_copy(0, 1 - my_c).wait_send()
    for s in shifts:
        for c in range(2):
            msg_line_copy(s, c).wait_send()
    for l in peers:
        msg_plane_copy(l).wait_send()
    if passing:
        @pl.when(passes)
        def _():
            for s in (1, 2):
                for k in range(CHUNKS):
                    pass_copy(s, k).wait_send()

        @pl.when(my_z != 3)
        def _():
            for k in range(CHUNKS):
                line_copy(1, k).wait_send()

        @pl.when(my_z == 3)
        def _():
            for k in range(CHUNKS):
                line_copy(2, k).wait_send()
    else:
        for s in shifts:
            for k in range(CHUNKS):
                line_copy(s, k).wait_send()
    if tie:
        if not passing:
            @pl.when(tie_send)
            def _():
                for k in range(CHUNKS):
                    line_copy(tie, k).wait_send()

        @pl.when(tie_recv)
        def _():
            for k in range(CHUNKS):
                pair_copy(tie, k).wait_send()
            for c in range(2):
                msg_line_copy(tie, c).wait_send()


def shards(segments, exclusion):
    rows, seg_len = segments.shape
    n_row = lax.axis_size("row")
    n_col = lax.axis_size("col")
    slots = n_col // 4 + 1
    dma = pltpu.SemaphoreType.DMA
    return pl.pallas_call(
        functools.partial(kernel, n_row, n_col),
        out_shape=jax.ShapeDtypeStruct((2, rows), jnp.float32),
        in_specs=[
            pl.BlockSpec(memory_space=pl.ANY),
            pl.BlockSpec(memory_space=pltpu.SMEM),
        ],
        out_specs=pl.BlockSpec(memory_space=pltpu.VMEM),
        scratch_shapes=[
            pltpu.VMEM((rows, seg_len), jnp.float32),
            dma((CHUNKS,)),
            pltpu.VMEM((n_row, rows, seg_len), jnp.bfloat16),
            pltpu.VMEM((slots, 2 * rows, seg_len), jnp.bfloat16),
            pltpu.VMEM((slots, 2, 8, 2 * rows), jnp.float32),
            pltpu.VMEM((n_row, 2, rows, 128), jnp.float32),
            pltpu.VMEM((2, 2 * rows, 128), jnp.float32),
            pltpu.VMEM((n_row, 2, 8, rows), jnp.float32),
            pltpu.VMEM((slots, 2, 2, rows), jnp.float32),
            pltpu.VMEM((slots, 2, 2, rows), jnp.float32),
            pltpu.VMEM((n_row, 2, rows), jnp.float32),
            pltpu.VMEM((n_row, 2, rows), jnp.float32),
            dma((n_row, CHUNKS)),
            dma((slots, 2, CHUNKS)),
            dma((n_row,)),
            dma((slots, 2)),
            dma((CHUNKS * n_row,)),
            dma((slots, CHUNKS)),
            dma((slots, CHUNKS)),
            dma((2, CHUNKS)),
            dma((n_row,)),
            dma((slots, 2)),
        ],
        compiler_params=pltpu.CompilerParams(
            collective_id=0, has_side_effects=True, vmem_limit_bytes=55900000
        ),
        cost_estimate=pl.CostEstimate(
            flops=2 * rows * 2 * rows * n_row * seg_len * slots,
            bytes_accessed=rows * seg_len * 4,
            transcendentals=0,
        ),
    )(segments, exclusion)


def solution(mesh):
    return jax.shard_map(
        shards,
        mesh=mesh,
        in_specs=(P(("row", "col"), None), P()),
        out_specs=P(None, ("row", "col")),
        check_vma=False,
    )
```

```python
import functools
import math

import jax
import jax.numpy as jnp
from jax import lax
from jax.experimental import pallas as pl
from jax.experimental.pallas import tpu as pltpu
from jax.sharding import PartitionSpec as P

MESH = pl.DeviceIdType.MESH
NONE = -3.0
CHUNKS = 4
TILE = 256


def kernel(
    n_row, n_col, seg_hbm, exclusion_ref, out_ref, seg_ref, in_sem, plane, line, line_acc,
    plane_acc, tie_rows, tie_cols, line_out, line_in, plane_out, plane_in, plane_recv, line_recv,
    msg_plane_recv, msg_line_recv, data_send, line_send, pair_send, pass_send, msg_plane_send,
    msg_line_send,
):
    rows, seg_len = seg_ref.shape
    n_z = n_col // 2
    step = rows // CHUNKS
    my_l = lax.axis_index("row")
    my_col = lax.axis_index("col")
    my_z = my_col // 2
    my_c = my_col % 2
    loads = [
        pltpu.make_async_copy(
            seg_hbm.at[pl.ds(k * step, step), :], seg_ref.at[pl.ds(k * step, step), :], in_sem.at[k]
        )
        for k in range(CHUNKS)
    ]
    for load in loads:
        load.start()
    shifts = list(range(1, (n_z - 1) // 2 + 1))
    tie = n_z // 2 if n_z % 2 == 0 else 0
    upper = my_z // max(tie, 1)
    tie_recv = (my_z % max(tie, 1) + upper) % 2 == 1
    tie_send = (my_z % max(tie, 1) + upper) % 2 == 0
    forwarding = n_row == 4
    passing = n_z == 4
    passes = my_z == 1
    if forwarding:
        x_peer = my_l + 1 - 2 * (my_l % 2)
        y_peer = my_l + 2 - 4 * (my_l // 2)
        peers = [x_peer, y_peer, 3 - my_l]
    else:
        peers = [(my_l + o) % n_row for o in range(1, n_row)]

    def device(l, z, c):
        return (l, z * 2 + c)

    barrier = pltpu.get_barrier_semaphore()
    sibling = device(my_l, my_z, 1 - my_c)
    greeted = [sibling] + [device(l, my_z, my_c) for l in peers]
    for d in range(1, n_z):
        greeted.append(device(my_l, (my_z + d) % n_z, my_c))
        greeted.append(device(my_l, (my_z + d) % n_z, 1 - my_c))
    for target in greeted:
        pl.semaphore_signal(barrier, inc=1, device_id=target, device_id_type=MESH)

    def half(c, k):
        return pl.ds(pl.multiple_of(c * rows + k * step, 16), step)

    def normalise(k):
        loads[k].wait()
        span = pl.ds(k * step, step)
        samples = seg_ref[span, :]
        average = jnp.mean(samples, axis=1, keepdims=True)
        centered = samples - average
        spread_inv = lax.rsqrt(jnp.mean(centered * centered, axis=1, keepdims=True) + 1e-05) * (
            1.0 / math.sqrt(seg_len)
        )
        normed = (centered * spread_inv).astype(jnp.bfloat16)
        plane[my_l, span, :] = normed
        line[0, half(my_c, k), :] = normed

    started = []

    def plane_copy(l, k, send_sem, target):
        part = plane.at[l, pl.ds(k * step, step), :]
        return pltpu.make_async_remote_copy(
            src_ref=part, dst_ref=part, send_sem=send_sem,
            recv_sem=plane_recv.at[l, k], device_id=target, device_id_type=MESH,
        )

    def send_part(l, k, target):
        copy = plane_copy(l, k, data_send.at[len(started)], device(target, my_z, my_c))
        copy.start()
        started.append(copy)

    def await_part(l, k):
        plane_copy(l, k, data_send.at[0], sibling).wait_recv()

    def line_copy(s, k):
        return pltpu.make_async_remote_copy(
            src_ref=plane.at[my_l, pl.ds(k * step, step), :], dst_ref=line.at[s, half(my_c, k), :],
            send_sem=line_send.at[s, k], recv_sem=line_recv.at[s, my_c, k],
            device_id=device(my_l, (my_z + s) % n_z, my_c), device_id_type=MESH,
        )

    def pair_copy(s, k):
        part = line.at[s, half(my_c, k), :]
        return pltpu.make_async_remote_copy(
            src_ref=part, dst_ref=part, send_sem=pair_send.at[s, k],
            recv_sem=line_recv.at[s, my_c, k], device_id=sibling, device_id_type=MESH,
        )

    def await_line(s, c, k):
        part = line.at[s, half(c, k), :]
        pltpu.make_async_remote_copy(
            src_ref=part, dst_ref=part, send_sem=pair_send.at[s, k],
            recv_sem=line_recv.at[s, c, k], device_id=sibling, device_id_type=MESH,
        ).wait_recv()

    def pass_copy(s, k):
        return pltpu.make_async_remote_copy(
            src_ref=line.at[s, half(my_c, k), :], dst_ref=line.at[3 - s, half(my_c, k), :],
            send_sem=pass_send.at[s - 1, k], recv_sem=line_recv.at[3 - s, my_c, k],
            device_id=device(my_l, 4 - 2 * s, my_c), device_id_type=MESH,
        )

    def take_line(s, k):
        await_line(s, my_c, k)
        pair_copy(s, k).start()

    normalise(0)
    pl.semaphore_wait(barrier, len(greeted))
    for k in range(CHUNKS):
        if k:
            normalise(k)
        if passing:
            pl.when(my_z != 3)(lambda: line_copy(1, k).start())
            pl.when(my_z == 3)(lambda: line_copy(2, k).start())
        else:
            for s in shifts:
                line_copy(s, k).start()
    for k in range(CHUNKS):
        for l in peers[:2] if forwarding else peers:
            send_part(my_l, k, l)
    for k in range(CHUNKS):
        pair_copy(0, k).start()
    if tie and not passing:
        @pl.when(tie_send)
        def _():
            for k in range(CHUNKS):
                line_copy(tie, k).start()

    line_acc[...] = jnp.full(line_acc.shape, NONE, jnp.float32)
    plane_acc[...] = jnp.full(plane_acc.shape, NONE, jnp.float32)
    tie_rows[...] = jnp.full(tie_rows.shape, NONE, jnp.float32)
    tie_cols[...] = jnp.full(tie_cols.shape, NONE, jnp.float32)
    exclude = exclusion_ref[0]

    def dot(a, b):
        return lax.dot_general(
            a, b, (((1,), (1,)), ((), ())), preferred_element_type=jnp.float32
        )

    def lanes(values):
        best = values[:, :128]
        for g in range(1, values.shape[1] // 128):
            best = jnp.maximum(best, values[:, g * 128 : (g + 1) * 128])
        return best

    def sublanes(values):
        return jnp.max(values.reshape(values.shape[0] // 8, 8, values.shape[1]), axis=0)

    def gap_of(s, l):
        return (l - my_l) * n_z + my_z - (my_z + n_z - s) % n_z

    def block(s, l):
        gap = gap_of(s, l)

        def keep(side, cols, values):
            line_acc[s, side, :, cols] = jnp.maximum(line_acc[s, side, :, cols], sublanes(values))
            if s:
                plane_acc[l, 1 - side] = jnp.maximum(plane_acc[l, 1 - side], lanes(values))

        def masked():
            for begin in range(0, 2 * rows, TILE):
                cols = pl.ds(begin, TILE)
                p = dot(plane[l], line[s, cols, :])
                apart = (gap * 2 * rows + my_c * rows - begin) + (
                    lax.broadcasted_iota(jnp.int32, p.shape, 0)
                    - lax.broadcasted_iota(jnp.int32, p.shape, 1)
                )
                keep(1, cols, jnp.where(apart > exclude, p, NONE))
                keep(0, cols, jnp.where(apart < -exclude, p, NONE))

        def plain():
            side = (gap > 0).astype(jnp.int32)
            for begin in range(0, 2 * rows, TILE):
                cols = pl.ds(begin, TILE)
                keep(side, cols, dot(plane[l], line[s, cols, :]))

        if s == 0:
            masked() if n_z == 1 or l is my_l else plain()
        elif min(s, n_z - s) == 1:
            near = (gap >= -1) & (gap <= 1)
            pl.when(near)(masked)
            pl.when(jnp.logical_not(near))(plain)
        else:
            plain()

    for k in range(CHUNKS):
        await_line(0, 1 - my_c, k)
    block(0, my_l)
    early, late = (peers[:2], peers[2:]) if forwarding else (peers, [])
    for k in range(CHUNKS):
        if passing:
            @pl.when(passes)
            def _():
                await_line(1, my_c, k)
                pass_copy(1, k).start()
                pair_copy(1, k).start()

        if forwarding and k < CHUNKS // 2:
            await_part(x_peer, k)
            send_part(x_peer, k, y_peer)
    if forwarding:
        for k in range(CHUNKS // 2, CHUNKS):
            await_part(y_peer, k)
            send_part(y_peer, k, x_peer)
    for k in range(CHUNKS):
        if passing:
            @pl.when(passes)
            def _():
                take_line(2, k)
                pass_copy(2, k).start()

        if not forwarding:
            for l in early:
                await_part(l, k)
    if forwarding:
        for k in range(CHUNKS // 2):
            await_part(x_peer, k + CHUNKS // 2)
            await_part(y_peer, k)
    for l in early:
        block(0, l)
    for s in shifts:
        for k in range(CHUNKS):
            if passing:
                pl.when(jnp.logical_not(passes))(functools.partial(take_line, s, k))
            else:
                take_line(s, k)
        for k in range(CHUNKS):
            await_line(s, 1 - my_c, k)
        for l in [my_l] + early:
            block(s, l)
    for l in late:
        for k in range(CHUNKS):
            await_part(l, k)
        for s in [0] + shifts:
            block(s, l)

    def msg_line_copy(s, c):
        return pltpu.make_async_remote_copy(
            src_ref=line_out.at[s, c], dst_ref=line_in.at[s, my_c],
            send_sem=msg_line_send.at[s, c], recv_sem=msg_line_recv.at[s, my_c],
            device_id=device(my_l, (my_z + n_z - s) % n_z, c), device_id_type=MESH,
        )

    def await_msg_line(s, c):
        pltpu.make_async_remote_copy(
            src_ref=line_out.at[s, c], dst_ref=line_in.at[s, c],
            send_sem=msg_line_send.at[s, c], recv_sem=msg_line_recv.at[s, c],
            device_id=sibling, device_id_type=MESH,
        ).wait_recv()

    for s in [0] + shifts:
        for side in range(2):
            best = jnp.max(line_acc[s, side], axis=0, keepdims=True)
            for c in range(2):
                line_out[s, c, side : side + 1, :] = best[:, c * rows : (c + 1) * rows]
        for c in (my_c, 1 - my_c) if s else (1 - my_c,):
            msg_line_copy(s, c).start()
    if shifts:
        for l in range(n_row):
            for side in range(2):
                plane_out[l, side : side + 1, :] = jnp.max(
                    plane_acc[l, side].T, axis=0, keepdims=True
                )
    else:
        plane_out[...] = jnp.full(plane_out.shape, NONE, jnp.float32)

    if tie:
        @pl.when(tie_recv)
        def _():
            done = 0
            for k in range(CHUNKS):
                if passing:
                    pl.when(jnp.logical_not(passes))(functools.partial(take_line, tie, k))
                else:
                    take_line(tie, k)
                await_line(tie, 1 - my_c, k)
                spans = [pl.ds(c * rows + k * step, step) for c in range(2)]
                data = jnp.concatenate([line[tie, span, :] for span in spans], axis=0)
                for l in range(n_row):
                    p = dot(data, plane[l])
                    gap = gap_of(tie, l)

                    def keep(side, line_values, plane_values):
                        best = lanes(line_values)
                        for c, span in enumerate(spans):
                            tie_rows[side, span, :] = jnp.maximum(
                                tie_rows[side, span, :], best[c * step : (c + 1) * step]
                            )
                        tie_cols[l, 1 - side] = jnp.maximum(
                            tie_cols[l, 1 - side], sublanes(plane_values)
                        )

                    if min(tie, n_z - tie) == 1:
                        index = lax.broadcasted_iota(jnp.int32, p.shape, 0)
                        index = jnp.where(index >= step, index + (rows - step), index) + k * step
                        apart = (gap * 2 * rows + my_c * rows) + (
                            lax.broadcasted_iota(jnp.int32, p.shape, 1) - index
                        )
                        later = jnp.where(apart > exclude, p, NONE)
                        earlier = jnp.where(apart < -exclude, p, NONE)
                        keep(1, later, later)
                        keep(0, earlier, earlier)
                    else:
                        keep((gap > 0).astype(jnp.int32), p, p)
                upto = (k + 1) * step // 128 * 128
                if upto > done:
                    for c in range(2):
                        for side in range(2):
                            line_out[tie, c, side : side + 1, done:upto] = jnp.max(
                                tie_rows[side, c * rows + done : c * rows + upto, :].T,
                                axis=0, keepdims=True,
                            )
                    done = upto
            for c in (my_c, 1 - my_c):
                msg_line_copy(tie, c).start()
            for l in range(n_row):
                for side in range(2):
                    plane_out[l, side : side + 1, :] = jnp.maximum(
                        plane_out[l, side : side + 1, :],
                        jnp.max(tie_cols[l, side], axis=0, keepdims=True),
                    )

    def msg_plane_copy(l):
        return pltpu.make_async_remote_copy(
            src_ref=plane_out.at[l], dst_ref=plane_in.at[my_l],
            send_sem=msg_plane_send.at[l], recv_sem=msg_plane_recv.at[my_l],
            device_id=device(l, my_z, my_c), device_id_type=MESH,
        )

    def await_msg_plane(l):
        pltpu.make_async_remote_copy(
            src_ref=plane_out.at[l], dst_ref=plane_in.at[l],
            send_sem=msg_plane_send.at[l], recv_sem=msg_plane_recv.at[l],
            device_id=sibling, device_id_type=MESH,
        ).wait_recv()

    for l in peers:
        msg_plane_copy(l).start()
    best = jnp.maximum(line_out[0, my_c], plane_out[my_l])
    await_msg_line(0, 1 - my_c)
    best = jnp.maximum(best, line_in[0, 1 - my_c])
    for s in shifts:
        for c in range(2):
            await_msg_line(s, c)
            best = jnp.maximum(best, line_in[s, c])
    for l in peers:
        await_msg_plane(l)
        best = jnp.maximum(best, plane_in[l])
    out_ref[...] = 1.0 - best
    if tie:
        @pl.when(tie_send)
        def _():
            for c in range(2):
                await_msg_line(tie, c)
            out_ref[...] = jnp.minimum(
                out_ref[...], 1.0 - jnp.maximum(line_in[tie, 0], line_in[tie, 1])
            )

    for copy in started:
        copy.wait_send()
    for k in range(CHUNKS):
        pair_copy(0, k).wait_send()
        for s in shifts:
            pair_copy(s, k).wait_send()
    msg_line_copy(0, 1 - my_c).wait_send()
    for s in shifts:
        for c in range(2):
            msg_line_copy(s, c).wait_send()
    for l in peers:
        msg_plane_copy(l).wait_send()
    if passing:
        @pl.when(passes)
        def _():
            for s in (1, 2):
                for k in range(CHUNKS):
                    pass_copy(s, k).wait_send()

        @pl.when(my_z != 3)
        def _():
            for k in range(CHUNKS):
                line_copy(1, k).wait_send()

        @pl.when(my_z == 3)
        def _():
            for k in range(CHUNKS):
                line_copy(2, k).wait_send()
    else:
        for s in shifts:
            for k in range(CHUNKS):
                line_copy(s, k).wait_send()
    if tie:
        if not passing:
            @pl.when(tie_send)
            def _():
                for k in range(CHUNKS):
                    line_copy(tie, k).wait_send()

        @pl.when(tie_recv)
        def _():
            for k in range(CHUNKS):
                pair_copy(tie, k).wait_send()
            for c in range(2):
                msg_line_copy(tie, c).wait_send()


def shards(segments, exclusion):
    rows, seg_len = segments.shape
    n_row = lax.axis_size("row")
    n_col = lax.axis_size("col")
    slots = n_col // 4 + 1
    dma = pltpu.SemaphoreType.DMA
    return pl.pallas_call(
        functools.partial(kernel, n_row, n_col),
        out_shape=jax.ShapeDtypeStruct((2, rows), jnp.float32),
        in_specs=[
            pl.BlockSpec(memory_space=pl.ANY),
            pl.BlockSpec(memory_space=pltpu.SMEM),
        ],
        out_specs=pl.BlockSpec(memory_space=pltpu.VMEM),
        scratch_shapes=[
            pltpu.VMEM((rows, seg_len), jnp.float32),
            dma((CHUNKS,)),
            pltpu.VMEM((n_row, rows, seg_len), jnp.bfloat16),
            pltpu.VMEM((slots, 2 * rows, seg_len), jnp.bfloat16),
            pltpu.VMEM((slots, 2, 8, 2 * rows), jnp.float32),
            pltpu.VMEM((n_row, 2, rows, 128), jnp.float32),
            pltpu.VMEM((2, 2 * rows, 128), jnp.float32),
            pltpu.VMEM((n_row, 2, 8, rows), jnp.float32),
            pltpu.VMEM((slots, 2, 2, rows), jnp.float32),
            pltpu.VMEM((slots, 2, 2, rows), jnp.float32),
            pltpu.VMEM((n_row, 2, rows), jnp.float32),
            pltpu.VMEM((n_row, 2, rows), jnp.float32),
            dma((n_row, CHUNKS)),
            dma((slots, 2, CHUNKS)),
            dma((n_row,)),
            dma((slots, 2)),
            dma((CHUNKS * n_row,)),
            dma((slots, CHUNKS)),
            dma((slots, CHUNKS)),
            dma((2, CHUNKS)),
            dma((n_row,)),
            dma((slots, 2)),
        ],
        compiler_params=pltpu.CompilerParams(
            collective_id=0, has_side_effects=True, vmem_limit_bytes=55900000
        ),
        cost_estimate=pl.CostEstimate(
            flops=2 * rows * 2 * rows * n_row * seg_len * slots,
            bytes_accessed=rows * seg_len * 4,
            transcendentals=0,
        ),
    )(segments, exclusion)


def solution(mesh):
    return jax.shard_map(
        shards,
        mesh=mesh,
        in_specs=(P(("row", "col"), None), P()),
        out_specs=P(None, ("row", "col")),
        check_vma=False,
    )
```

```python
import functools
import math

import jax
import jax.numpy as jnp
from jax import lax
from jax.experimental import pallas as pl
from jax.experimental.pallas import tpu as pltpu
from jax.sharding import PartitionSpec as P

MESH = pl.DeviceIdType.MESH
NONE = -3.0
CHUNKS = 4
PARTS = 3
TILE = 256


def kernel(
    n_row, n_col, seg_hbm, exclusion_ref, out_ref, seg_ref, in_sem, plane, line, line_acc,
    plane_acc, tie_acc, line_out, line_in, plane_out, plane_in, plane_recv, line_recv,
    msg_plane_recv, msg_line_recv, data_send, line_send, pair_send, pass_send, msg_plane_send,
    msg_line_send,
):
    rows, seg_len = seg_ref.shape
    n_z = n_col // 2
    step = rows // CHUNKS
    size = rows // PARTS
    my_l = lax.axis_index("row")
    my_col = lax.axis_index("col")
    my_z = my_col // 2
    my_c = my_col % 2
    loads = [
        pltpu.make_async_copy(
            seg_hbm.at[pl.ds(k * size, size), :], seg_ref.at[pl.ds(k * size, size), :], in_sem.at[k]
        )
        for k in range(PARTS)
    ]
    for load in loads:
        load.start()
    shifts = list(range(1, (n_z - 1) // 2 + 1))
    tie = n_z // 2 if n_z % 2 == 0 else 0
    upper = my_z // max(tie, 1)
    tie_recv = (my_z % max(tie, 1) + upper) % 2 == 1
    tie_send = (my_z % max(tie, 1) + upper) % 2 == 0
    forwarding = n_row == 4
    passing = n_z == 4
    passes = my_z == 1
    if forwarding:
        x_peer = my_l + 1 - 2 * (my_l % 2)
        y_peer = my_l + 2 - 4 * (my_l // 2)
        peers = [x_peer, y_peer, 3 - my_l]
    else:
        peers = [(my_l + o) % n_row for o in range(1, n_row)]

    def device(l, z, c):
        return (l, z * 2 + c)

    barrier = pltpu.get_barrier_semaphore()
    sibling = device(my_l, my_z, 1 - my_c)
    greeted = [sibling] + [device(l, my_z, my_c) for l in peers]
    for d in range(1, n_z):
        greeted.append(device(my_l, (my_z + d) % n_z, my_c))
        greeted.append(device(my_l, (my_z + d) % n_z, 1 - my_c))
    for target in greeted:
        pl.semaphore_signal(barrier, inc=1, device_id=target, device_id_type=MESH)

    def half(c, k):
        return pl.ds(pl.multiple_of(c * rows + k * size, 16), size)

    def normalise(k):
        loads[k].wait()
        span = pl.ds(k * size, size)
        samples = seg_ref[span, :]
        average = jnp.mean(samples, axis=1, keepdims=True)
        centered = samples - average
        spread_inv = lax.rsqrt(jnp.mean(centered * centered, axis=1, keepdims=True) + 1e-05) * (
            1.0 / math.sqrt(seg_len)
        )
        normed = (centered * spread_inv).astype(jnp.bfloat16)
        plane[span, :] = normed
        line[0, half(my_c, k), :] = normed

    started = []

    order = [my_l] + peers

    def back(j):
        return j if forwarding else (n_row - j) % n_row

    def plane_copy(src, dst, k, send_sem, target):
        return pltpu.make_async_remote_copy(
            src_ref=plane.at[pl.ds(src * rows + k * step, step), :],
            dst_ref=plane.at[pl.ds(dst * rows + k * step, step), :],
            send_sem=send_sem, recv_sem=plane_recv.at[dst, k],
            device_id=target, device_id_type=MESH,
        )

    def send_part(src, dst, k, j):
        copy = plane_copy(
            src, dst, k, data_send.at[len(started)], device(order[j], my_z, my_c)
        )
        copy.start()
        started.append(copy)

    def await_part(j, k):
        plane_copy(j, j, k, data_send.at[0], sibling).wait_recv()

    def line_copy(s, k):
        return pltpu.make_async_remote_copy(
            src_ref=plane.at[pl.ds(k * size, size), :], dst_ref=line.at[s, half(my_c, k), :],
            send_sem=line_send.at[s, k], recv_sem=line_recv.at[s, my_c, k],
            device_id=device(my_l, (my_z + s) % n_z, my_c), device_id_type=MESH,
        )

    def pair_copy(s, k):
        part = line.at[s, half(my_c, k), :]
        return pltpu.make_async_remote_copy(
            src_ref=part, dst_ref=part, send_sem=pair_send.at[s, k],
            recv_sem=line_recv.at[s, my_c, k], device_id=sibling, device_id_type=MESH,
        )

    def await_line(s, c, k):
        part = line.at[s, half(c, k), :]
        pltpu.make_async_remote_copy(
            src_ref=part, dst_ref=part, send_sem=pair_send.at[s, k],
            recv_sem=line_recv.at[s, c, k], device_id=sibling, device_id_type=MESH,
        ).wait_recv()

    def pass_copy(s, k):
        return pltpu.make_async_remote_copy(
            src_ref=line.at[s, half(my_c, k), :], dst_ref=line.at[3 - s, half(my_c, k), :],
            send_sem=pass_send.at[s - 1, k], recv_sem=line_recv.at[3 - s, my_c, k],
            device_id=device(my_l, 4 - 2 * s, my_c), device_id_type=MESH,
        )

    def take_line(s, k):
        await_line(s, my_c, k)
        pair_copy(s, k).start()

    normalise(0)
    pl.semaphore_wait(barrier, len(greeted))
    sent = 0
    for k in range(PARTS):
        if k:
            normalise(k)
        if passing:
            pl.when(my_z != 3)(lambda: line_copy(1, k).start())
            pl.when(my_z == 3)(lambda: line_copy(2, k).start())
        else:
            for s in shifts:
                line_copy(s, k).start()
        while (sent + 1) * step <= (k + 1) * size:
            for j in (1, 2) if forwarding else range(1, n_row):
                send_part(0, back(j), sent, j)
            sent += 1
        pair_copy(0, k).start()
    if tie and not passing:
        @pl.when(tie_send)
        def _():
            for k in range(PARTS):
                line_copy(tie, k).start()

    line_acc[...] = jnp.full(line_acc.shape, NONE, jnp.float32)
    plane_acc[...] = jnp.full(plane_acc.shape, NONE, jnp.float32)
    tie_acc[...] = jnp.full(tie_acc.shape, NONE, jnp.float32)
    exclude = exclusion_ref[0]

    def dot(a, b):
        return lax.dot_general(
            a, b, (((1,), (1,)), ((), ())), preferred_element_type=jnp.float32
        )

    def lanes(values):
        best = values[:, :128]
        for g in range(1, values.shape[1] // 128):
            best = jnp.maximum(best, values[:, g * 128 : (g + 1) * 128])
        return best

    def sublanes(values):
        return jnp.max(values.reshape(values.shape[0] // 8, 8, values.shape[1]), axis=0)

    def gap_of(s, l):
        return (l - my_l) * n_z + my_z - (my_z + n_z - s) % n_z

    def rows_of(j):
        return plane[j * rows : (j + 1) * rows, :]

    def block(s, j):
        gap = gap_of(s, order[j])

        def keep(side, cols, values):
            line_acc[s, side, :, cols] = jnp.maximum(line_acc[s, side, :, cols], sublanes(values))
            if s:
                plane_acc[j, 1 - side] = jnp.maximum(plane_acc[j, 1 - side], lanes(values))

        def masked():
            for begin in range(0, 2 * rows, TILE):
                cols = pl.ds(begin, TILE)
                p = dot(rows_of(j), line[s, cols, :])
                apart = (gap * 2 * rows + my_c * rows - begin) + (
                    lax.broadcasted_iota(jnp.int32, p.shape, 0)
                    - lax.broadcasted_iota(jnp.int32, p.shape, 1)
                )
                keep(1, cols, jnp.where(apart > exclude, p, NONE))
                keep(0, cols, jnp.where(apart < -exclude, p, NONE))

        def plain():
            side = (gap > 0).astype(jnp.int32)
            for begin in range(0, 2 * rows, TILE):
                cols = pl.ds(begin, TILE)
                keep(side, cols, dot(rows_of(j), line[s, cols, :]))

        if s == 0:
            masked() if n_z == 1 or j == 0 else plain()
        elif min(s, n_z - s) == 1:
            near = (gap >= -1) & (gap <= 1)
            pl.when(near)(masked)
            pl.when(jnp.logical_not(near))(plain)
        else:
            plain()

    def pass_on(k):
        if passing:
            @pl.when(my_z != 0)
            def _():
                take_line(1, k)

            @pl.when(passes)
            def _():
                pass_copy(1, k).start()
                take_line(2, k)
                pass_copy(2, k).start()

    for k in range(PARTS):
        await_line(0, 1 - my_c, k)
    block(0, 0)
    if forwarding:
        for k in range(CHUNKS):
            await_part(1, k)
            if k < CHUNKS // 2:
                send_part(1, 3, k, 2)
            await_part(2, k)
            if k >= CHUNKS // 2:
                send_part(2, 3, k, 1)
            if k < PARTS:
                pass_on(k)
        early, late = [1, 2], [3]
    else:
        early, late = list(range(1, n_row)), []
        for j in early:
            for k in range(CHUNKS):
                await_part(j, k)
        for k in range(PARTS):
            pass_on(k)
    for j in early:
        block(0, j)
    for s in shifts:
        for k in range(PARTS):
            if passing:
                pl.when(my_z == 0)(functools.partial(take_line, s, k))
            else:
                take_line(s, k)
        for k in range(PARTS):
            await_line(s, 1 - my_c, k)
        for j in [0] + early:
            block(s, j)
    for j in late:
        for k in range(CHUNKS):
            await_part(j, k)
        for s in [0] + shifts:
            block(s, j)

    def msg_line_copy(s, c):
        return pltpu.make_async_remote_copy(
            src_ref=line_out.at[s, c], dst_ref=line_in.at[s, my_c],
            send_sem=msg_line_send.at[s, c], recv_sem=msg_line_recv.at[s, my_c],
            device_id=device(my_l, (my_z + n_z - s) % n_z, c), device_id_type=MESH,
        )

    def await_msg_line(s, c):
        pltpu.make_async_remote_copy(
            src_ref=line_out.at[s, c], dst_ref=line_in.at[s, c],
            send_sem=msg_line_send.at[s, c], recv_sem=msg_line_recv.at[s, c],
            device_id=sibling, device_id_type=MESH,
        ).wait_recv()

    def send_line_maxima(s):
        for side in range(2):
            best = jnp.max(line_acc[s, side], axis=0, keepdims=True)
            for c in range(2):
                line_out[s, c, side : side + 1, :] = best[:, c * rows : (c + 1) * rows]
        for c in (my_c, 1 - my_c) if s else (1 - my_c,):
            msg_line_copy(s, c).start()

    for s in [0] + shifts:
        send_line_maxima(s)
    if shifts:
        for l in range(n_row):
            for side in range(2):
                plane_out[l, side : side + 1, :] = jnp.max(
                    plane_acc[l, side].T, axis=0, keepdims=True
                )
    else:
        plane_out[...] = jnp.full(plane_out.shape, NONE, jnp.float32)

    if tie:
        @pl.when(tie_recv)
        def _():
            adjacent = n_z == 2
            for k in range(PARTS):
                if passing:
                    pl.when(jnp.logical_not(passes))(functools.partial(take_line, tie, k))
                else:
                    take_line(tie, k)
                await_line(tie, 1 - my_c, k)
                spans = [pl.ds(c * rows + k * size, size) for c in range(2)]
                data = jnp.concatenate([line[tie, span, :] for span in spans], axis=0)
                products = dot(plane[...], data)
                for j in range(n_row):
                    p = products[j * rows : (j + 1) * rows]
                    gap = gap_of(tie, order[j])

                    def keep(side, slot, values):
                        best = sublanes(values)
                        for c, span in enumerate(spans):
                            line_acc[tie, side, :, span] = jnp.maximum(
                                line_acc[tie, side, :, span], best[:, c * size : (c + 1) * size]
                            )
                        tie_acc[j, slot] = jnp.maximum(tie_acc[j, slot], lanes(values))

                    if adjacent:
                        index = lax.broadcasted_iota(jnp.int32, p.shape, 1)
                        index = jnp.where(index >= size, index + (rows - size), index) + k * size
                        apart = (gap * 2 * rows + my_c * rows) + (
                            lax.broadcasted_iota(jnp.int32, p.shape, 0) - index
                        )
                        keep(1, 0, jnp.where(apart > exclude, p, NONE))
                        keep(0, 1, jnp.where(apart < -exclude, p, NONE))
                    else:
                        keep((gap > 0).astype(jnp.int32), 0, p)
            send_line_maxima(tie)
            for j in range(n_row):
                for slot in range(2 if adjacent else 1):
                    side = slot if adjacent else 1 - (gap_of(tie, order[j]) > 0).astype(jnp.int32)
                    best = jnp.max(tie_acc[j, slot].T, axis=0, keepdims=True)
                    plane_out[j, pl.ds(side, 1), :] = jnp.maximum(
                        plane_out[j, pl.ds(side, 1), :], best
                    )

    def msg_plane_copy(j):
        return pltpu.make_async_remote_copy(
            src_ref=plane_out.at[j], dst_ref=plane_in.at[back(j)],
            send_sem=msg_plane_send.at[j], recv_sem=msg_plane_recv.at[back(j)],
            device_id=device(order[j], my_z, my_c), device_id_type=MESH,
        )

    def await_msg_plane(j):
        pltpu.make_async_remote_copy(
            src_ref=plane_out.at[j], dst_ref=plane_in.at[j],
            send_sem=msg_plane_send.at[j], recv_sem=msg_plane_recv.at[j],
            device_id=sibling, device_id_type=MESH,
        ).wait_recv()

    for j in range(1, n_row):
        msg_plane_copy(j).start()
    best = jnp.maximum(line_out[0, my_c], plane_out[0])
    await_msg_line(0, 1 - my_c)
    best = jnp.maximum(best, line_in[0, 1 - my_c])
    for s in shifts:
        for c in range(2):
            await_msg_line(s, c)
            best = jnp.maximum(best, line_in[s, c])
    for j in range(1, n_row):
        await_msg_plane(j)
        best = jnp.maximum(best, plane_in[j])
    out_ref[...] = 1.0 - best
    if tie:
        @pl.when(tie_send)
        def _():
            for c in range(2):
                await_msg_line(tie, c)
            out_ref[...] = jnp.minimum(
                out_ref[...], 1.0 - jnp.maximum(line_in[tie, 0], line_in[tie, 1])
            )

    for copy in started:
        copy.wait_send()
    for k in range(PARTS):
        pair_copy(0, k).wait_send()
        for s in shifts:
            pair_copy(s, k).wait_send()
    msg_line_copy(0, 1 - my_c).wait_send()
    for s in shifts:
        for c in range(2):
            msg_line_copy(s, c).wait_send()
    for j in range(1, n_row):
        msg_plane_copy(j).wait_send()
    if passing:
        @pl.when(passes)
        def _():
            for s in (1, 2):
                for k in range(PARTS):
                    pass_copy(s, k).wait_send()

        @pl.when(my_z != 3)
        def _():
            for k in range(PARTS):
                line_copy(1, k).wait_send()

        @pl.when(my_z == 3)
        def _():
            for k in range(PARTS):
                line_copy(2, k).wait_send()
    else:
        for s in shifts:
            for k in range(PARTS):
                line_copy(s, k).wait_send()
    if tie:
        if not passing:
            @pl.when(tie_send)
            def _():
                for k in range(PARTS):
                    line_copy(tie, k).wait_send()

        @pl.when(tie_recv)
        def _():
            for k in range(PARTS):
                pair_copy(tie, k).wait_send()
            for c in range(2):
                msg_line_copy(tie, c).wait_send()


def shards(segments, exclusion):
    rows, seg_len = segments.shape
    n_row = lax.axis_size("row")
    n_col = lax.axis_size("col")
    slots = n_col // 4 + 1
    dma = pltpu.SemaphoreType.DMA
    return pl.pallas_call(
        functools.partial(kernel, n_row, n_col),
        out_shape=jax.ShapeDtypeStruct((2, rows), jnp.float32),
        in_specs=[
            pl.BlockSpec(memory_space=pl.ANY),
            pl.BlockSpec(memory_space=pltpu.SMEM),
        ],
        out_specs=pl.BlockSpec(memory_space=pltpu.VMEM),
        scratch_shapes=[
            pltpu.VMEM((rows, seg_len), jnp.float32),
            dma((PARTS,)),
            pltpu.VMEM((n_row * rows, seg_len), jnp.bfloat16),
            pltpu.VMEM((slots, 2 * rows, seg_len), jnp.bfloat16),
            pltpu.VMEM((slots, 2, 8, 2 * rows), jnp.float32),
            pltpu.VMEM((n_row, 2, rows, 128), jnp.float32),
            pltpu.VMEM((n_row, 2, rows, 128), jnp.float32),
            pltpu.VMEM((slots, 2, 2, rows), jnp.float32),
            pltpu.VMEM((slots, 2, 2, rows), jnp.float32),
            pltpu.VMEM((n_row, 2, rows), jnp.float32),
            pltpu.VMEM((n_row, 2, rows), jnp.float32),
            dma((n_row, CHUNKS)),
            dma((slots, 2, PARTS)),
            dma((n_row,)),
            dma((slots, 2)),
            dma((CHUNKS * n_row,)),
            dma((slots, PARTS)),
            dma((slots, PARTS)),
            dma((2, PARTS)),
            dma((n_row,)),
            dma((slots, 2)),
        ],
        compiler_params=pltpu.CompilerParams(
            collective_id=0, has_side_effects=True, vmem_limit_bytes=55900000
        ),
        cost_estimate=pl.CostEstimate(
            flops=2 * rows * 2 * rows * n_row * seg_len * slots,
            bytes_accessed=rows * seg_len * 4,
            transcendentals=0,
        ),
    )(segments, exclusion)


def solution(mesh):
    return jax.shard_map(
        shards,
        mesh=mesh,
        in_specs=(P(("row", "col"), None), P()),
        out_specs=P(None, ("row", "col")),
        check_vma=False,
    )
```

```python
import functools
import math

import jax
import jax.numpy as jnp
from jax import lax
from jax.experimental import pallas as pl
from jax.experimental.pallas import tpu as pltpu
from jax.sharding import PartitionSpec as P

MESH = pl.DeviceIdType.MESH
NONE = -3.0
CHUNKS = 4
PARTS = 3
TILE = 256


def kernel(
    n_row, n_col, seg_hbm, exclusion_ref, out_ref, seg_ref, in_sem, plane, line, line_acc,
    plane_acc, tie_acc, line_out, line_in, plane_out, plane_in, plane_recv, line_recv,
    msg_plane_recv, msg_line_recv, data_send, line_send, pair_send, pass_send, msg_plane_send,
    msg_line_send,
):
    rows, seg_len = seg_ref.shape
    n_z = n_col // 2
    step = rows // CHUNKS
    size = rows // PARTS
    my_l = lax.axis_index("row")
    my_col = lax.axis_index("col")
    my_z = my_col // 2
    my_c = my_col % 2
    loads = [
        pltpu.make_async_copy(
            seg_hbm.at[pl.ds(k * size, size), :], seg_ref.at[pl.ds(k * size, size), :], in_sem.at[k]
        )
        for k in range(PARTS)
    ]
    for load in loads:
        load.start()
    shifts = list(range(1, (n_z - 1) // 2 + 1))
    tie = n_z // 2 if n_z % 2 == 0 else 0
    upper = my_z // max(tie, 1)
    tie_recv = (my_z % max(tie, 1) + upper) % 2 == 1
    tie_send = (my_z % max(tie, 1) + upper) % 2 == 0
    forwarding = n_row == 4
    passing = False
    passes = my_z == 1
    if forwarding:
        x_peer = my_l + 1 - 2 * (my_l % 2)
        y_peer = my_l + 2 - 4 * (my_l // 2)
        peers = [x_peer, y_peer, 3 - my_l]
    else:
        peers = [(my_l + o) % n_row for o in range(1, n_row)]

    def device(l, z, c):
        return (l, z * 2 + c)

    barrier = pltpu.get_barrier_semaphore()
    sibling = device(my_l, my_z, 1 - my_c)
    greeted = [sibling] + [device(l, my_z, my_c) for l in peers]
    for d in range(1, n_z):
        greeted.append(device(my_l, (my_z + d) % n_z, my_c))
        greeted.append(device(my_l, (my_z + d) % n_z, 1 - my_c))
    for target in greeted:
        pl.semaphore_signal(barrier, inc=1, device_id=target, device_id_type=MESH)

    def half(c, k):
        return pl.ds(pl.multiple_of(c * rows + k * size, 16), size)

    def normalise(k):
        loads[k].wait()
        span = pl.ds(k * size, size)
        samples = seg_ref[span, :]
        average = jnp.mean(samples, axis=1, keepdims=True)
        centered = samples - average
        spread_inv = lax.rsqrt(jnp.mean(centered * centered, axis=1, keepdims=True) + 1e-05) * (
            1.0 / math.sqrt(seg_len)
        )
        normed = (centered * spread_inv).astype(jnp.bfloat16)
        plane[span, :] = normed
        line[0, half(my_c, k), :] = normed

    started = []

    order = [my_l] + peers

    def back(j):
        return j if forwarding else (n_row - j) % n_row

    def plane_copy(src, dst, k, send_sem, target):
        return pltpu.make_async_remote_copy(
            src_ref=plane.at[pl.ds(src * rows + k * step, step), :],
            dst_ref=plane.at[pl.ds(dst * rows + k * step, step), :],
            send_sem=send_sem, recv_sem=plane_recv.at[dst, k],
            device_id=target, device_id_type=MESH,
        )

    def send_part(src, dst, k, j):
        copy = plane_copy(
            src, dst, k, data_send.at[len(started)], device(order[j], my_z, my_c)
        )
        copy.start()
        started.append(copy)

    def await_part(j, k):
        plane_copy(j, j, k, data_send.at[0], sibling).wait_recv()

    def line_copy(s, k):
        return pltpu.make_async_remote_copy(
            src_ref=plane.at[pl.ds(k * size, size), :], dst_ref=line.at[s, half(my_c, k), :],
            send_sem=line_send.at[s, k], recv_sem=line_recv.at[s, my_c, k],
            device_id=device(my_l, (my_z + s) % n_z, my_c), device_id_type=MESH,
        )

    def pair_copy(s, k):
        part = line.at[s, half(my_c, k), :]
        return pltpu.make_async_remote_copy(
            src_ref=part, dst_ref=part, send_sem=pair_send.at[s, k],
            recv_sem=line_recv.at[s, my_c, k], device_id=sibling, device_id_type=MESH,
        )

    def await_line(s, c, k):
        part = line.at[s, half(c, k), :]
        pltpu.make_async_remote_copy(
            src_ref=part, dst_ref=part, send_sem=pair_send.at[s, k],
            recv_sem=line_recv.at[s, c, k], device_id=sibling, device_id_type=MESH,
        ).wait_recv()

    def pass_copy(s, k):
        return pltpu.make_async_remote_copy(
            src_ref=line.at[s, half(my_c, k), :], dst_ref=line.at[3 - s, half(my_c, k), :],
            send_sem=pass_send.at[s - 1, k], recv_sem=line_recv.at[3 - s, my_c, k],
            device_id=device(my_l, 4 - 2 * s, my_c), device_id_type=MESH,
        )

    def take_line(s, k):
        await_line(s, my_c, k)
        pair_copy(s, k).start()

    normalise(0)
    pl.semaphore_wait(barrier, len(greeted))
    sent = 0
    for k in range(PARTS):
        if k:
            normalise(k)
        if passing:
            pl.when(my_z != 3)(lambda: line_copy(1, k).start())
            pl.when(my_z == 3)(lambda: line_copy(2, k).start())
        else:
            for s in shifts:
                line_copy(s, k).start()
        while (sent + 1) * step <= (k + 1) * size:
            for j in (1, 2) if forwarding else range(1, n_row):
                send_part(0, back(j), sent, j)
            sent += 1
        pair_copy(0, k).start()
    if tie and not passing:
        @pl.when(tie_send)
        def _():
            for k in range(PARTS):
                line_copy(tie, k).start()

    line_acc[...] = jnp.full(line_acc.shape, NONE, jnp.float32)
    plane_acc[...] = jnp.full(plane_acc.shape, NONE, jnp.float32)
    tie_acc[...] = jnp.full(tie_acc.shape, NONE, jnp.float32)
    exclude = exclusion_ref[0]

    def dot(a, b):
        return lax.dot_general(
            a, b, (((1,), (1,)), ((), ())), preferred_element_type=jnp.float32
        )

    def lanes(values):
        best = values[:, :128]
        for g in range(1, values.shape[1] // 128):
            best = jnp.maximum(best, values[:, g * 128 : (g + 1) * 128])
        return best

    def sublanes(values):
        return jnp.max(values.reshape(values.shape[0] // 8, 8, values.shape[1]), axis=0)

    def gap_of(s, l):
        return (l - my_l) * n_z + my_z - (my_z + n_z - s) % n_z

    def rows_of(j):
        return plane[j * rows : (j + 1) * rows, :]

    def block(s, j):
        gap = gap_of(s, order[j])

        def keep(side, cols, values):
            line_acc[s, side, :, cols] = jnp.maximum(line_acc[s, side, :, cols], sublanes(values))
            if s:
                plane_acc[j, 1 - side] = jnp.maximum(plane_acc[j, 1 - side], lanes(values))

        def masked():
            for begin in range(0, 2 * rows, TILE):
                cols = pl.ds(begin, TILE)
                p = dot(rows_of(j), line[s, cols, :])
                apart = (gap * 2 * rows + my_c * rows - begin) + (
                    lax.broadcasted_iota(jnp.int32, p.shape, 0)
                    - lax.broadcasted_iota(jnp.int32, p.shape, 1)
                )
                keep(1, cols, jnp.where(apart > exclude, p, NONE))
                keep(0, cols, jnp.where(apart < -exclude, p, NONE))

        def plain():
            side = (gap > 0).astype(jnp.int32)
            for begin in range(0, 2 * rows, TILE):
                cols = pl.ds(begin, TILE)
                keep(side, cols, dot(rows_of(j), line[s, cols, :]))

        if s == 0:
            masked() if n_z == 1 or j == 0 else plain()
        elif min(s, n_z - s) == 1:
            near = (gap >= -1) & (gap <= 1)
            pl.when(near)(masked)
            pl.when(jnp.logical_not(near))(plain)
        else:
            plain()

    def pass_on(k):
        if passing:
            @pl.when(my_z != 0)
            def _():
                take_line(1, k)

            @pl.when(passes)
            def _():
                pass_copy(1, k).start()
                take_line(2, k)
                pass_copy(2, k).start()

    for k in range(PARTS):
        await_line(0, 1 - my_c, k)
    block(0, 0)
    if forwarding:
        for k in range(CHUNKS):
            await_part(1, k)
            if k < CHUNKS // 2:
                send_part(1, 3, k, 2)
            await_part(2, k)
            if k >= CHUNKS // 2:
                send_part(2, 3, k, 1)
            if k < PARTS:
                pass_on(k)
        early, late = [1, 2], [3]
    else:
        early, late = list(range(1, n_row)), []
        for j in early:
            for k in range(CHUNKS):
                await_part(j, k)
        for k in range(PARTS):
            pass_on(k)
    for j in early:
        block(0, j)
    for s in shifts:
        for k in range(PARTS):
            if passing:
                pl.when(my_z == 0)(functools.partial(take_line, s, k))
            else:
                take_line(s, k)
        for k in range(PARTS):
            await_line(s, 1 - my_c, k)
        for j in [0] + early:
            block(s, j)
    for j in late:
        for k in range(CHUNKS):
            await_part(j, k)
        for s in [0] + shifts:
            block(s, j)

    def msg_line_copy(s, c):
        return pltpu.make_async_remote_copy(
            src_ref=line_out.at[s, c], dst_ref=line_in.at[s, my_c],
            send_sem=msg_line_send.at[s, c], recv_sem=msg_line_recv.at[s, my_c],
            device_id=device(my_l, (my_z + n_z - s) % n_z, c), device_id_type=MESH,
        )

    def await_msg_line(s, c):
        pltpu.make_async_remote_copy(
            src_ref=line_out.at[s, c], dst_ref=line_in.at[s, c],
            send_sem=msg_line_send.at[s, c], recv_sem=msg_line_recv.at[s, c],
            device_id=sibling, device_id_type=MESH,
        ).wait_recv()

    def send_line_maxima(s):
        for side in range(2):
            best = jnp.max(line_acc[s, side], axis=0, keepdims=True)
            for c in range(2):
                line_out[s, c, side : side + 1, :] = best[:, c * rows : (c + 1) * rows]
        for c in (my_c, 1 - my_c) if s else (1 - my_c,):
            msg_line_copy(s, c).start()

    for s in [0] + shifts:
        send_line_maxima(s)
    if shifts:
        for l in range(n_row):
            for side in range(2):
                plane_out[l, side : side + 1, :] = jnp.max(
                    plane_acc[l, side].T, axis=0, keepdims=True
                )
    else:
        plane_out[...] = jnp.full(plane_out.shape, NONE, jnp.float32)

    if tie:
        @pl.when(tie_recv)
        def _():
            adjacent = n_z == 2
            for k in range(PARTS):
                if passing:
                    pl.when(jnp.logical_not(passes))(functools.partial(take_line, tie, k))
                else:
                    take_line(tie, k)
                await_line(tie, 1 - my_c, k)
                spans = [pl.ds(c * rows + k * size, size) for c in range(2)]
                data = jnp.concatenate([line[tie, span, :] for span in spans], axis=0)
                products = dot(plane[...], data)
                for j in range(n_row):
                    p = products[j * rows : (j + 1) * rows]
                    gap = gap_of(tie, order[j])

                    def keep(side, slot, values):
                        best = sublanes(values)
                        for c, span in enumerate(spans):
                            line_acc[tie, side, :, span] = jnp.maximum(
                                line_acc[tie, side, :, span], best[:, c * size : (c + 1) * size]
                            )
                        tie_acc[j, slot] = jnp.maximum(tie_acc[j, slot], lanes(values))

                    if adjacent:
                        index = lax.broadcasted_iota(jnp.int32, p.shape, 1)
                        index = jnp.where(index >= size, index + (rows - size), index) + k * size
                        apart = (gap * 2 * rows + my_c * rows) + (
                            lax.broadcasted_iota(jnp.int32, p.shape, 0) - index
                        )
                        keep(1, 0, jnp.where(apart > exclude, p, NONE))
                        keep(0, 1, jnp.where(apart < -exclude, p, NONE))
                    else:
                        keep((gap > 0).astype(jnp.int32), 0, p)
            send_line_maxima(tie)
            for j in range(n_row):
                for slot in range(2 if adjacent else 1):
                    side = slot if adjacent else 1 - (gap_of(tie, order[j]) > 0).astype(jnp.int32)
                    best = jnp.max(tie_acc[j, slot].T, axis=0, keepdims=True)
                    plane_out[j, pl.ds(side, 1), :] = jnp.maximum(
                        plane_out[j, pl.ds(side, 1), :], best
                    )

    def msg_plane_copy(j):
        return pltpu.make_async_remote_copy(
            src_ref=plane_out.at[j], dst_ref=plane_in.at[back(j)],
            send_sem=msg_plane_send.at[j], recv_sem=msg_plane_recv.at[back(j)],
            device_id=device(order[j], my_z, my_c), device_id_type=MESH,
        )

    def await_msg_plane(j):
        pltpu.make_async_remote_copy(
            src_ref=plane_out.at[j], dst_ref=plane_in.at[j],
            send_sem=msg_plane_send.at[j], recv_sem=msg_plane_recv.at[j],
            device_id=sibling, device_id_type=MESH,
        ).wait_recv()

    for j in range(1, n_row):
        msg_plane_copy(j).start()
    best = jnp.maximum(line_out[0, my_c], plane_out[0])
    await_msg_line(0, 1 - my_c)
    best = jnp.maximum(best, line_in[0, 1 - my_c])
    for s in shifts:
        for c in range(2):
            await_msg_line(s, c)
            best = jnp.maximum(best, line_in[s, c])
    for j in range(1, n_row):
        await_msg_plane(j)
        best = jnp.maximum(best, plane_in[j])
    out_ref[...] = 1.0 - best
    if tie:
        @pl.when(tie_send)
        def _():
            for c in range(2):
                await_msg_line(tie, c)
            out_ref[...] = jnp.minimum(
                out_ref[...], 1.0 - jnp.maximum(line_in[tie, 0], line_in[tie, 1])
            )

    for copy in started:
        copy.wait_send()
    for k in range(PARTS):
        pair_copy(0, k).wait_send()
        for s in shifts:
            pair_copy(s, k).wait_send()
    msg_line_copy(0, 1 - my_c).wait_send()
    for s in shifts:
        for c in range(2):
            msg_line_copy(s, c).wait_send()
    for j in range(1, n_row):
        msg_plane_copy(j).wait_send()
    if passing:
        @pl.when(passes)
        def _():
            for s in (1, 2):
                for k in range(PARTS):
                    pass_copy(s, k).wait_send()

        @pl.when(my_z != 3)
        def _():
            for k in range(PARTS):
                line_copy(1, k).wait_send()

        @pl.when(my_z == 3)
        def _():
            for k in range(PARTS):
                line_copy(2, k).wait_send()
    else:
        for s in shifts:
            for k in range(PARTS):
                line_copy(s, k).wait_send()
    if tie:
        if not passing:
            @pl.when(tie_send)
            def _():
                for k in range(PARTS):
                    line_copy(tie, k).wait_send()

        @pl.when(tie_recv)
        def _():
            for k in range(PARTS):
                pair_copy(tie, k).wait_send()
            for c in range(2):
                msg_line_copy(tie, c).wait_send()


def shards(segments, exclusion):
    rows, seg_len = segments.shape
    n_row = lax.axis_size("row")
    n_col = lax.axis_size("col")
    slots = n_col // 4 + 1
    dma = pltpu.SemaphoreType.DMA
    return pl.pallas_call(
        functools.partial(kernel, n_row, n_col),
        out_shape=jax.ShapeDtypeStruct((2, rows), jnp.float32),
        in_specs=[
            pl.BlockSpec(memory_space=pl.ANY),
            pl.BlockSpec(memory_space=pltpu.SMEM),
        ],
        out_specs=pl.BlockSpec(memory_space=pltpu.VMEM),
        scratch_shapes=[
            pltpu.VMEM((rows, seg_len), jnp.float32),
            dma((PARTS,)),
            pltpu.VMEM((n_row * rows, seg_len), jnp.bfloat16),
            pltpu.VMEM((slots, 2 * rows, seg_len), jnp.bfloat16),
            pltpu.VMEM((slots, 2, 8, 2 * rows), jnp.float32),
            pltpu.VMEM((n_row, 2, rows, 128), jnp.float32),
            pltpu.VMEM((n_row, 2, rows, 128), jnp.float32),
            pltpu.VMEM((slots, 2, 2, rows), jnp.float32),
            pltpu.VMEM((slots, 2, 2, rows), jnp.float32),
            pltpu.VMEM((n_row, 2, rows), jnp.float32),
            pltpu.VMEM((n_row, 2, rows), jnp.float32),
            dma((n_row, CHUNKS)),
            dma((slots, 2, PARTS)),
            dma((n_row,)),
            dma((slots, 2)),
            dma((CHUNKS * n_row,)),
            dma((slots, PARTS)),
            dma((slots, PARTS)),
            dma((2, PARTS)),
            dma((n_row,)),
            dma((slots, 2)),
        ],
        compiler_params=pltpu.CompilerParams(
            collective_id=0, has_side_effects=True, vmem_limit_bytes=55900000
        ),
        cost_estimate=pl.CostEstimate(
            flops=2 * rows * 2 * rows * n_row * seg_len * slots,
            bytes_accessed=rows * seg_len * 4,
            transcendentals=0,
        ),
    )(segments, exclusion)


def solution(mesh):
    return jax.shard_map(
        shards,
        mesh=mesh,
        in_specs=(P(("row", "col"), None), P()),
        out_specs=P(None, ("row", "col")),
        check_vma=False,
    )
```

```python
import functools
import math

import jax
import jax.numpy as jnp
from jax import lax
from jax.experimental import pallas as pl
from jax.experimental.pallas import tpu as pltpu
from jax.sharding import PartitionSpec as P

MESH = pl.DeviceIdType.MESH
NONE = -3.0
CHUNKS = 2
PARTS = 3
TILE = 256


def kernel(
    n_row, n_col, seg_hbm, exclusion_ref, out_ref, seg_ref, in_sem, plane, line, line_acc,
    plane_acc, tie_acc, line_out, line_in, plane_out, plane_in, plane_recv, line_recv,
    msg_plane_recv, msg_line_recv, data_send, line_send, pair_send, pass_send, msg_plane_send,
    msg_line_send,
):
    rows, seg_len = seg_ref.shape
    n_z = n_col // 2
    step = rows // CHUNKS
    size = rows // PARTS
    my_l = lax.axis_index("row")
    my_col = lax.axis_index("col")
    my_z = my_col // 2
    my_c = my_col % 2
    loads = [
        pltpu.make_async_copy(
            seg_hbm.at[pl.ds(k * size, size), :], seg_ref.at[pl.ds(k * size, size), :], in_sem.at[k]
        )
        for k in range(PARTS)
    ]
    for load in loads:
        load.start()
    shifts = list(range(1, (n_z - 1) // 2 + 1))
    tie = n_z // 2 if n_z % 2 == 0 else 0
    upper = my_z // max(tie, 1)
    tie_recv = (my_z % max(tie, 1) + upper) % 2 == 1
    tie_send = (my_z % max(tie, 1) + upper) % 2 == 0
    forwarding = n_row == 4
    passing = False
    passes = my_z == 1
    if forwarding:
        x_peer = my_l + 1 - 2 * (my_l % 2)
        y_peer = my_l + 2 - 4 * (my_l // 2)
        peers = [x_peer, y_peer, 3 - my_l]
    else:
        peers = [(my_l + o) % n_row for o in range(1, n_row)]

    def device(l, z, c):
        return (l, z * 2 + c)

    barrier = pltpu.get_barrier_semaphore()
    sibling = device(my_l, my_z, 1 - my_c)
    greeted = [sibling] + [device(l, my_z, my_c) for l in peers]
    for d in range(1, n_z):
        greeted.append(device(my_l, (my_z + d) % n_z, my_c))
        greeted.append(device(my_l, (my_z + d) % n_z, 1 - my_c))
    for target in greeted:
        pl.semaphore_signal(barrier, inc=1, device_id=target, device_id_type=MESH)

    def half(c, k):
        return pl.ds(pl.multiple_of(c * rows + k * size, 16), size)

    def normalise(k):
        loads[k].wait()
        span = pl.ds(k * size, size)
        samples = seg_ref[span, :]
        average = jnp.mean(samples, axis=1, keepdims=True)
        centered = samples - average
        spread_inv = lax.rsqrt(jnp.mean(centered * centered, axis=1, keepdims=True) + 1e-05) * (
            1.0 / math.sqrt(seg_len)
        )
        normed = (centered * spread_inv).astype(jnp.bfloat16)
        plane[span, :] = normed
        line[0, half(my_c, k), :] = normed

    started = []

    order = [my_l] + peers

    def back(j):
        return j if forwarding else (n_row - j) % n_row

    def plane_copy(src, dst, k, send_sem, target):
        return pltpu.make_async_remote_copy(
            src_ref=plane.at[pl.ds(src * rows + k * step, step), :],
            dst_ref=plane.at[pl.ds(dst * rows + k * step, step), :],
            send_sem=send_sem, recv_sem=plane_recv.at[dst, k],
            device_id=target, device_id_type=MESH,
        )

    def send_part(src, dst, k, j):
        copy = plane_copy(
            src, dst, k, data_send.at[len(started)], device(order[j], my_z, my_c)
        )
        copy.start()
        started.append(copy)

    def await_part(j, k):
        plane_copy(j, j, k, data_send.at[0], sibling).wait_recv()

    def line_copy(s, k):
        return pltpu.make_async_remote_copy(
            src_ref=plane.at[pl.ds(k * size, size), :], dst_ref=line.at[s, half(my_c, k), :],
            send_sem=line_send.at[s, k], recv_sem=line_recv.at[s, my_c, k],
            device_id=device(my_l, (my_z + s) % n_z, my_c), device_id_type=MESH,
        )

    def pair_copy(s, k):
        part = line.at[s, half(my_c, k), :]
        return pltpu.make_async_remote_copy(
            src_ref=part, dst_ref=part, send_sem=pair_send.at[s, k],
            recv_sem=line_recv.at[s, my_c, k], device_id=sibling, device_id_type=MESH,
        )

    def await_line(s, c, k):
        part = line.at[s, half(c, k), :]
        pltpu.make_async_remote_copy(
            src_ref=part, dst_ref=part, send_sem=pair_send.at[s, k],
            recv_sem=line_recv.at[s, c, k], device_id=sibling, device_id_type=MESH,
        ).wait_recv()

    def pass_copy(s, k):
        return pltpu.make_async_remote_copy(
            src_ref=line.at[s, half(my_c, k), :], dst_ref=line.at[3 - s, half(my_c, k), :],
            send_sem=pass_send.at[s - 1, k], recv_sem=line_recv.at[3 - s, my_c, k],
            device_id=device(my_l, 4 - 2 * s, my_c), device_id_type=MESH,
        )

    def take_line(s, k):
        await_line(s, my_c, k)
        pair_copy(s, k).start()

    normalise(0)
    pl.semaphore_wait(barrier, len(greeted))
    sent = 0
    for k in range(PARTS):
        if k:
            normalise(k)
        if passing:
            pl.when(my_z != 3)(lambda: line_copy(1, k).start())
            pl.when(my_z == 3)(lambda: line_copy(2, k).start())
        else:
            for s in shifts:
                line_copy(s, k).start()
        while (sent + 1) * step <= (k + 1) * size:
            for j in (1, 2) if forwarding else range(1, n_row):
                send_part(0, back(j), sent, j)
            sent += 1
        pair_copy(0, k).start()
    if tie and not passing:
        @pl.when(tie_send)
        def _():
            for k in range(PARTS):
                line_copy(tie, k).start()

    line_acc[...] = jnp.full(line_acc.shape, NONE, jnp.float32)
    plane_acc[...] = jnp.full(plane_acc.shape, NONE, jnp.float32)
    tie_acc[...] = jnp.full(tie_acc.shape, NONE, jnp.float32)
    exclude = exclusion_ref[0]

    def dot(a, b):
        return lax.dot_general(
            a, b, (((1,), (1,)), ((), ())), preferred_element_type=jnp.float32
        )

    def lanes(values):
        best = values[:, :128]
        for g in range(1, values.shape[1] // 128):
            best = jnp.maximum(best, values[:, g * 128 : (g + 1) * 128])
        return best

    def sublanes(values):
        return jnp.max(values.reshape(values.shape[0] // 8, 8, values.shape[1]), axis=0)

    def gap_of(s, l):
        return (l - my_l) * n_z + my_z - (my_z + n_z - s) % n_z

    def rows_of(j):
        return plane[j * rows : (j + 1) * rows, :]

    def block(s, j):
        gap = gap_of(s, order[j])

        def keep(side, cols, values):
            line_acc[s, side, :, cols] = jnp.maximum(line_acc[s, side, :, cols], sublanes(values))
            if s:
                plane_acc[j, 1 - side] = jnp.maximum(plane_acc[j, 1 - side], lanes(values))

        def masked():
            for begin in range(0, 2 * rows, TILE):
                cols = pl.ds(begin, TILE)
                p = dot(rows_of(j), line[s, cols, :])
                apart = (gap * 2 * rows + my_c * rows - begin) + (
                    lax.broadcasted_iota(jnp.int32, p.shape, 0)
                    - lax.broadcasted_iota(jnp.int32, p.shape, 1)
                )
                keep(1, cols, jnp.where(apart > exclude, p, NONE))
                keep(0, cols, jnp.where(apart < -exclude, p, NONE))

        def plain():
            side = (gap > 0).astype(jnp.int32)
            for begin in range(0, 2 * rows, TILE):
                cols = pl.ds(begin, TILE)
                keep(side, cols, dot(rows_of(j), line[s, cols, :]))

        if s == 0:
            masked() if n_z == 1 or j == 0 else plain()
        elif min(s, n_z - s) == 1:
            near = (gap >= -1) & (gap <= 1)
            pl.when(near)(masked)
            pl.when(jnp.logical_not(near))(plain)
        else:
            plain()

    def pass_on(k):
        if passing:
            @pl.when(my_z != 0)
            def _():
                take_line(1, k)

            @pl.when(passes)
            def _():
                pass_copy(1, k).start()
                take_line(2, k)
                pass_copy(2, k).start()

    for k in range(PARTS):
        await_line(0, 1 - my_c, k)
    block(0, 0)
    if forwarding:
        for k in range(CHUNKS):
            await_part(1, k)
            if k < CHUNKS // 2:
                send_part(1, 3, k, 2)
            await_part(2, k)
            if k >= CHUNKS // 2:
                send_part(2, 3, k, 1)
            if k < PARTS:
                pass_on(k)
        early, late = [1, 2], [3]
    else:
        early, late = list(range(1, n_row)), []
        for j in early:
            for k in range(CHUNKS):
                await_part(j, k)
        for k in range(PARTS):
            pass_on(k)
    for j in early:
        block(0, j)
    for s in shifts:
        for k in range(PARTS):
            if passing:
                pl.when(my_z == 0)(functools.partial(take_line, s, k))
            else:
                take_line(s, k)
        for k in range(PARTS):
            await_line(s, 1 - my_c, k)
        for j in [0] + early:
            block(s, j)
    for j in late:
        for k in range(CHUNKS):
            await_part(j, k)
        for s in [0] + shifts:
            block(s, j)

    def msg_line_copy(s, c):
        return pltpu.make_async_remote_copy(
            src_ref=line_out.at[s, c], dst_ref=line_in.at[s, my_c],
            send_sem=msg_line_send.at[s, c], recv_sem=msg_line_recv.at[s, my_c],
            device_id=device(my_l, (my_z + n_z - s) % n_z, c), device_id_type=MESH,
        )

    def await_msg_line(s, c):
        pltpu.make_async_remote_copy(
            src_ref=line_out.at[s, c], dst_ref=line_in.at[s, c],
            send_sem=msg_line_send.at[s, c], recv_sem=msg_line_recv.at[s, c],
            device_id=sibling, device_id_type=MESH,
        ).wait_recv()

    def send_line_maxima(s):
        for side in range(2):
            best = jnp.max(line_acc[s, side], axis=0, keepdims=True)
            for c in range(2):
                line_out[s, c, side : side + 1, :] = best[:, c * rows : (c + 1) * rows]
        for c in (my_c, 1 - my_c) if s else (1 - my_c,):
            msg_line_copy(s, c).start()

    for s in [0] + shifts:
        send_line_maxima(s)
    if shifts:
        for l in range(n_row):
            for side in range(2):
                plane_out[l, side : side + 1, :] = jnp.max(
                    plane_acc[l, side].T, axis=0, keepdims=True
                )
    else:
        plane_out[...] = jnp.full(plane_out.shape, NONE, jnp.float32)

    if tie:
        @pl.when(tie_recv)
        def _():
            adjacent = n_z == 2
            for k in range(PARTS):
                if passing:
                    pl.when(jnp.logical_not(passes))(functools.partial(take_line, tie, k))
                else:
                    take_line(tie, k)
                await_line(tie, 1 - my_c, k)
                spans = [pl.ds(c * rows + k * size, size) for c in range(2)]
                data = jnp.concatenate([line[tie, span, :] for span in spans], axis=0)
                products = dot(plane[...], data)
                for j in range(n_row):
                    p = products[j * rows : (j + 1) * rows]
                    gap = gap_of(tie, order[j])

                    def keep(side, slot, values):
                        best = sublanes(values)
                        for c, span in enumerate(spans):
                            line_acc[tie, side, :, span] = jnp.maximum(
                                line_acc[tie, side, :, span], best[:, c * size : (c + 1) * size]
                            )
                        tie_acc[j, slot] = jnp.maximum(tie_acc[j, slot], lanes(values))

                    if adjacent:
                        index = lax.broadcasted_iota(jnp.int32, p.shape, 1)
                        index = jnp.where(index >= size, index + (rows - size), index) + k * size
                        apart = (gap * 2 * rows + my_c * rows) + (
                            lax.broadcasted_iota(jnp.int32, p.shape, 0) - index
                        )
                        keep(1, 0, jnp.where(apart > exclude, p, NONE))
                        keep(0, 1, jnp.where(apart < -exclude, p, NONE))
                    else:
                        keep((gap > 0).astype(jnp.int32), 0, p)
            send_line_maxima(tie)
            for j in range(n_row):
                for slot in range(2 if adjacent else 1):
                    side = slot if adjacent else 1 - (gap_of(tie, order[j]) > 0).astype(jnp.int32)
                    best = jnp.max(tie_acc[j, slot].T, axis=0, keepdims=True)
                    plane_out[j, pl.ds(side, 1), :] = jnp.maximum(
                        plane_out[j, pl.ds(side, 1), :], best
                    )

    def msg_plane_copy(j):
        return pltpu.make_async_remote_copy(
            src_ref=plane_out.at[j], dst_ref=plane_in.at[back(j)],
            send_sem=msg_plane_send.at[j], recv_sem=msg_plane_recv.at[back(j)],
            device_id=device(order[j], my_z, my_c), device_id_type=MESH,
        )

    def await_msg_plane(j):
        pltpu.make_async_remote_copy(
            src_ref=plane_out.at[j], dst_ref=plane_in.at[j],
            send_sem=msg_plane_send.at[j], recv_sem=msg_plane_recv.at[j],
            device_id=sibling, device_id_type=MESH,
        ).wait_recv()

    for j in range(1, n_row):
        msg_plane_copy(j).start()
    best = jnp.maximum(line_out[0, my_c], plane_out[0])
    await_msg_line(0, 1 - my_c)
    best = jnp.maximum(best, line_in[0, 1 - my_c])
    for s in shifts:
        for c in range(2):
            await_msg_line(s, c)
            best = jnp.maximum(best, line_in[s, c])
    for j in range(1, n_row):
        await_msg_plane(j)
        best = jnp.maximum(best, plane_in[j])
    out_ref[...] = 1.0 - best
    if tie:
        @pl.when(tie_send)
        def _():
            for c in range(2):
                await_msg_line(tie, c)
            out_ref[...] = jnp.minimum(
                out_ref[...], 1.0 - jnp.maximum(line_in[tie, 0], line_in[tie, 1])
            )

    for copy in started:
        copy.wait_send()
    for k in range(PARTS):
        pair_copy(0, k).wait_send()
        for s in shifts:
            pair_copy(s, k).wait_send()
    msg_line_copy(0, 1 - my_c).wait_send()
    for s in shifts:
        for c in range(2):
            msg_line_copy(s, c).wait_send()
    for j in range(1, n_row):
        msg_plane_copy(j).wait_send()
    if passing:
        @pl.when(passes)
        def _():
            for s in (1, 2):
                for k in range(PARTS):
                    pass_copy(s, k).wait_send()

        @pl.when(my_z != 3)
        def _():
            for k in range(PARTS):
                line_copy(1, k).wait_send()

        @pl.when(my_z == 3)
        def _():
            for k in range(PARTS):
                line_copy(2, k).wait_send()
    else:
        for s in shifts:
            for k in range(PARTS):
                line_copy(s, k).wait_send()
    if tie:
        if not passing:
            @pl.when(tie_send)
            def _():
                for k in range(PARTS):
                    line_copy(tie, k).wait_send()

        @pl.when(tie_recv)
        def _():
            for k in range(PARTS):
                pair_copy(tie, k).wait_send()
            for c in range(2):
                msg_line_copy(tie, c).wait_send()


def shards(segments, exclusion):
    rows, seg_len = segments.shape
    n_row = lax.axis_size("row")
    n_col = lax.axis_size("col")
    slots = n_col // 4 + 1
    dma = pltpu.SemaphoreType.DMA
    return pl.pallas_call(
        functools.partial(kernel, n_row, n_col),
        out_shape=jax.ShapeDtypeStruct((2, rows), jnp.float32),
        in_specs=[
            pl.BlockSpec(memory_space=pl.ANY),
            pl.BlockSpec(memory_space=pltpu.SMEM),
        ],
        out_specs=pl.BlockSpec(memory_space=pltpu.VMEM),
        scratch_shapes=[
            pltpu.VMEM((rows, seg_len), jnp.float32),
            dma((PARTS,)),
            pltpu.VMEM((n_row * rows, seg_len), jnp.bfloat16),
            pltpu.VMEM((slots, 2 * rows, seg_len), jnp.bfloat16),
            pltpu.VMEM((slots, 2, 8, 2 * rows), jnp.float32),
            pltpu.VMEM((n_row, 2, rows, 128), jnp.float32),
            pltpu.VMEM((n_row, 2, rows, 128), jnp.float32),
            pltpu.VMEM((slots, 2, 2, rows), jnp.float32),
            pltpu.VMEM((slots, 2, 2, rows), jnp.float32),
            pltpu.VMEM((n_row, 2, rows), jnp.float32),
            pltpu.VMEM((n_row, 2, rows), jnp.float32),
            dma((n_row, CHUNKS)),
            dma((slots, 2, PARTS)),
            dma((n_row,)),
            dma((slots, 2)),
            dma((CHUNKS * n_row,)),
            dma((slots, PARTS)),
            dma((slots, PARTS)),
            dma((2, PARTS)),
            dma((n_row,)),
            dma((slots, 2)),
        ],
        compiler_params=pltpu.CompilerParams(
            collective_id=0, has_side_effects=True, vmem_limit_bytes=55900000
        ),
        cost_estimate=pl.CostEstimate(
            flops=2 * rows * 2 * rows * n_row * seg_len * slots,
            bytes_accessed=rows * seg_len * 4,
            transcendentals=0,
        ),
    )(segments, exclusion)


def solution(mesh):
    return jax.shard_map(
        shards,
        mesh=mesh,
        in_specs=(P(("row", "col"), None), P()),
        out_specs=P(None, ("row", "col")),
        check_vma=False,
    )
```
